32 devices in a mesh: groups: 2 (over x), ctx: 8 (over z, y), head: 2 (over core).
Axes of the slice: x: 2, y: 2, z: 4, core: 2. Of those that a mesh axis runs over, the one named last changes fastest.
Arguments:
- query_nope: bfloat16 [32, 128, 128], P('groups', ('ctx', 'head')), parts along dimension 0, may hold values from -6 to 6
- query_rope: bfloat16 [32, 8192], P('groups', ('ctx', 'head')), parts along dimension 0, may hold values from -31 to 31
- key_absorb: bfloat16 [128, 128, 512], P(('ctx', 'head')), may hold values from -0.5 to 0.5
- value_absorb: bfloat16 [128, 512, 128], P(('ctx', 'head')), may hold values from -4 to 4
- output_weight: bfloat16 [16384, 7168], P(('ctx', 'head')), may hold values from -0.0625 to 0.0625
- latent_cache: bfloat16 [3584, 64, 576], P(('groups', 'ctx')), parts along dimension 0, may hold values from -4 to 4
- page_owner: int32 [3584], P(('groups', 'ctx')), parts along dimension 0, may hold values from -1 to 15, as said below
Outputs:
- layer_output: bfloat16 [32, 7168], P('groups', ('ctx', 'head')), parts along dimension 0
The draws below stay inside these ranges and needn't reach their ends.
There are 2 independent parts, one for each index of `groups`. The reference program is written for one: setup_inputs(seed, part) draws one part's arguments, and reference() takes and returns one part's arrays. A program takes and returns all parts, laid end to end along the dimension named above; an argument that names none is the same for every part. Nothing has to cross between parts.
Inputs may be any that keep to these rules, and one draw needn't show every extreme that they name: `page_owner`: a slot's request, or -1 for an unused slot; every request owns at least one slot; every index of ctx has an eighth of its 224 slots or more in use, and some index has all 224 in use.
All inputs are finite; a program needn't handle non-finite values.
Results may differ from the reference program's by a relative error of at most 0.03.
Values may be sent and summed in bfloat16 or wider, within the bound.
No kernel may reach another device: no remote copies, remote signals or barrier semaphores. Data moves between devices by JAX's collectives and lax.ppermute only.
A program may use at most 128 MiB of HBM per device.

```python
import jax
import jax.numpy as jnp
from jax import lax

D = 7168
H = 128
DN = 128
DR = 64
LAT = 512
DV = 128
PAGE = 64
BLOCK_PAGES = 8
R = 16
PAGES_DEV = 224
POOL = 1792
KV = 576


def load_pattern():
    device_count = POOL // PAGES_DEV
    lowest = PAGES_DEV // 8
    spread = max(device_count - 1, 1)
    return [lowest + (PAGES_DEV - lowest) * device * device // (spread * spread) for device in range(device_count)]


def page_layout(key):
    pattern = load_pattern()
    filled = sum(pattern)
    device_count = len(pattern)
    shuffled = jax.random.permutation(jax.random.fold_in(key, 11), device_count)
    device_load = jnp.array(pattern, jnp.int32)[shuffled]
    slot_ids = jnp.arange(POOL, dtype=jnp.int32)
    in_use = slot_ids % PAGES_DEV < device_load[slot_ids // PAGES_DEV]
    ranked = jnp.clip(jnp.cumsum(in_use.astype(jnp.int32)) - 1, 0, filled - 1)
    logical = jax.random.permutation(jax.random.fold_in(key, 13), filled).astype(jnp.int32)[ranked]
    boundary = jnp.sort(jax.random.permutation(jax.random.fold_in(key, 12), filled - 1).astype(jnp.int32)[:R - 1] + 1)
    owners = jnp.sum((logical[:, None] >= boundary[None, :]).astype(jnp.int32), axis=1)
    return jnp.where(in_use, owners, -1).astype(jnp.int32)


def draw_page_owner(key, part):
    owners = page_layout(key)
    return owners


def draw_latent_cache(key, part):
    latent = jax.random.truncated_normal(jax.random.fold_in(key, 21), -4.0, 4.0, (POOL, PAGE, LAT), jnp.float32)
    rope_part = jax.random.truncated_normal(jax.random.fold_in(key, 22), -4.0, 4.0, (POOL, PAGE, DR), jnp.float32)
    return jnp.concatenate([latent, rope_part], axis=2).astype(jnp.bfloat16)


def draw_query_rope(key, part):
    values = jax.random.truncated_normal(jax.random.fold_in(key, 32), -4.0, 4.0, (R, H, DR), jnp.float32)
    return values.reshape(R, H * DR).astype(jnp.bfloat16)


def strengthened(drawn, key, source, target, shards_of, factor):
    owner, partner = [(jnp.arange(drawn.shape[dim]) // (drawn.shape[dim] // shards_of)).reshape([-1 if axis == dim else 1 for axis in range(drawn.ndim)]) for dim in (source, target)]
    chosen = jax.random.permutation(key, shards_of)[partner]
    strong = (owner == chosen) | (owner == (partner + shards_of // 2) % shards_of)
    return jnp.where(strong, factor * drawn, drawn)


def block_scale(own_key, shape, cuts, low, high):
    factor_of, own = 1.0, jax.random.fold_in(own_key, 6)
    for dim, blocks in cuts:
        heights = jnp.exp(jax.random.uniform(jax.random.fold_in(own, dim), (blocks,), jnp.float32, low / len(cuts), high / len(cuts)))
        factor_of = factor_of * jnp.repeat(heights, shape[dim] // blocks).reshape([-1 if axis == dim else 1 for axis in range(len(shape))])
    return factor_of


def normal_values(own_key, extent, scale, bound, split=(), kind=jnp.bfloat16):
    values = jax.random.normal(own_key, extent, jnp.float32) * scale
    if len(split) > 0:
        values = block_scale(own_key, extent, split, -0.22, 0.18) * values
    return jnp.clip(values, min=-bound, max=bound).astype(kind)


def noise_with(rng, dims, scale, limit, cuts, heavy, held_as=jnp.bfloat16):
    values = scale * jax.random.normal(rng, dims, jnp.float32)
    if cuts:
        values = values * block_scale(rng, dims, cuts, -0.22, 0.18)
    return jnp.clip(strengthened(values, jax.random.fold_in(rng, 3), *heavy), -limit, limit).astype(held_as)


def setup_inputs(seed: int = 0, part: int = 0) -> dict:
    keys = jax.random.split(jax.random.key(seed), 8)
    own_keys = jax.random.split(jax.random.fold_in(keys[7], part), 8)
    query_nope = normal_values(own_keys[0], (R, H, DN), 1.0, 6.0, ((1, 16),))
    query_rope = draw_query_rope(jax.random.fold_in(jax.random.fold_in(keys[7], part), 71), part)
    key_absorb = normal_values(keys[2], (H, DN, LAT), DN ** -0.5, 0.5, ((0, 16),))
    value_absorb = normal_values(keys[3], (H, LAT, DV), 0.7, 4.0, ((0, 16),))
    output_weight = noise_with(keys[4], (H * DV, D), (H * DV) ** -0.5, 0.0625, ((0, 16),), (0, 1, 16, 2.0))
    latent_cache = draw_latent_cache(jax.random.fold_in(jax.random.fold_in(keys[7], part), 71), part)
    page_owner = draw_page_owner(jax.random.fold_in(jax.random.fold_in(keys[7], part), 71), part)
    return {"query_nope": query_nope, "query_rope": query_rope, "key_absorb": key_absorb, "value_absorb": value_absorb, "output_weight": output_weight, "latent_cache": latent_cache, "page_owner": page_owner}


masked_score = -1.0e30
highest = lax.Precision.HIGHEST


def reference(query_nope, query_rope, key_absorb, value_absorb, output_weight, latent_cache, page_owner):
    score_scale = (DN + DR) ** -0.5
    query_latent = jnp.einsum("rhn,hnl->rhl", query_nope.astype(jnp.float32), key_absorb.astype(jnp.float32), precision=highest).astype(jnp.bfloat16)
    query_full = jnp.concatenate([query_latent, query_rope.reshape(R, H, DR)], axis=2)
    block_count = POOL // BLOCK_PAGES
    cache_blocks = latent_cache.reshape(block_count, BLOCK_PAGES, PAGE, KV)
    owner_blocks = page_owner.reshape(block_count, BLOCK_PAGES)

    def score_block(inputs):
        page_rows, owner_ids = inputs
        page_query = query_full[jnp.clip(owner_ids, 0, R - 1)]
        scores = jnp.einsum("ptk,phk->pth", page_rows.astype(jnp.float32), page_query.astype(jnp.float32), precision=highest) * score_scale
        return jnp.where((owner_ids >= 0)[:, None, None], scores, masked_score)

    block_scores = lax.map(score_block, (cache_blocks, owner_blocks))
    page_max = jnp.max(block_scores, axis=2).reshape(POOL, H)
    owner_hot = page_owner[:, None] == jnp.arange(R, dtype=jnp.int32)[None, :]
    row_max = jnp.max(jnp.where(owner_hot[:, :, None], page_max[:, None, :], masked_score), axis=0)

    def sum_block(state, inputs):
        running_sum, running_total = state
        page_rows, owner_ids, scores = inputs
        onehot = (owner_ids[:, None] == jnp.arange(R, dtype=jnp.int32)[None, :]).astype(jnp.float32)
        offset = row_max[jnp.clip(owner_ids, 0, R - 1)]
        weights = jnp.where((owner_ids >= 0)[:, None, None], jnp.exp(scores - offset[:, None, :]), 0.0)
        weight_half = weights.astype(jnp.bfloat16).astype(jnp.float32)
        page_out = jnp.einsum("pth,ptl->phl", weight_half, page_rows[:, :, :LAT].astype(jnp.float32), precision=highest)
        running_sum = running_sum + jnp.einsum("pr,phl->rhl", onehot, page_out, precision=highest)
        running_total = running_total + jnp.einsum("pr,ph->rh", onehot, jnp.sum(weights, axis=1), precision=highest)
        return (running_sum, running_total), None

    start_state = (jnp.zeros((R, H, LAT), jnp.float32), jnp.zeros((R, H), jnp.float32))
    (latent_sum, total), _ = lax.scan(sum_block, start_state, (cache_blocks, owner_blocks, block_scores))
    attended = (latent_sum / total[:, :, None]).astype(jnp.bfloat16)
    head_out = jnp.einsum("rhl,hlv->rhv", attended.astype(jnp.float32), value_absorb.astype(jnp.float32), precision=highest).astype(jnp.bfloat16)
    return jnp.dot(head_out.reshape(R, H * DV), output_weight, preferred_element_type=jnp.float32).astype(jnp.bfloat16)
```

```python
import functools

import jax
import jax.numpy as jnp
from jax import lax
from jax.experimental import pallas as pl
from jax.experimental.pallas import tpu as pltpu
from jax.sharding import PartitionSpec as P

masked_score = -1e30


def ring_order(count):
    if count % 2:
        return list(range(count))
    return list(range(0, count, 2)) + list(range(count - 1, 0, -2))


def attend_kernel(
    score_scale, group_pages, owner_ref, place_ref, query_ref, cache_ref, out_ref, stat_ref,
    score_scr, max_scr, total_scr, sum_scr,
):
    requests, heads, entry_size = query_ref.shape
    pages, page_len, _ = cache_ref.shape
    latent_size = out_ref.shape[3]
    blocks, _, heads_here, _ = out_ref.shape
    pair_len = 2 * page_len
    pair_count = group_pages // 2
    groups = pages // group_pages
    first_half = lax.broadcasted_iota(jnp.int32, (heads, pair_len), 1) < page_len

    for r in range(requests + 1):
        max_scr[r] = jnp.full((heads, pair_len), masked_score, jnp.float32)
        total_scr[r] = jnp.zeros((heads, pair_len), jnp.float32)
        sum_scr[r] = jnp.zeros((heads, latent_size), jnp.float32)

    def owners_of(g):
        raw = [owner_ref[g * group_pages + k] for k in range(group_pages)]
        return [jnp.where(o < 0, requests, o) for o in raw]

    def score_group(g, carry):
        owners = owners_of(g)
        keys = cache_ref[pl.ds(g * group_pages, group_pages)].reshape(
            group_pages * page_len, entry_size
        )
        queries = jnp.concatenate(
            [query_ref[jnp.minimum(o, requests - 1)] for o in owners], axis=0
        )
        scores = (
            lax.dot_general(
                queries, keys, (((1,), (1,)), ((), ())), preferred_element_type=jnp.float32
            )
            * score_scale
        )
        for p in range(pair_count):
            left, right = 2 * p, 2 * p + 1
            columns = slice(p * pair_len, (p + 1) * pair_len)
            pair = jnp.where(
                first_half,
                scores[left * heads : (left + 1) * heads, columns],
                scores[right * heads : (right + 1) * heads, columns],
            )
            score_scr[g * pair_count + p] = pair
            max_scr[owners[left]] = jnp.maximum(
                max_scr[owners[left]], jnp.where(first_half, pair, masked_score)
            )
            max_scr[owners[right]] = jnp.maximum(
                max_scr[owners[right]], jnp.where(first_half, masked_score, pair)
            )
        return carry

    lax.fori_loop(0, groups, score_group, 0, unroll=2)

    for r in range(requests + 1):
        top = jnp.max(max_scr[r], axis=1, keepdims=True)
        max_scr[r] = jnp.broadcast_to(top, (heads, pair_len))

    def sum_group(g, carry):
        owners = owners_of(g)
        values = cache_ref[pl.ds(g * group_pages, group_pages)].reshape(
            group_pages * page_len, entry_size
        )[:, :latent_size]
        rows = []
        for p in range(pair_count):
            left, right = owners[2 * p], owners[2 * p + 1]
            offset = jnp.where(first_half, max_scr[left], max_scr[right])
            weight = jnp.exp(score_scr[g * pair_count + p] - offset)
            left_weight = jnp.where(first_half, weight, 0.0)
            right_weight = jnp.where(first_half, 0.0, weight)
            total_scr[left] += left_weight
            total_scr[right] += right_weight
            for part in (left_weight, right_weight):
                half = part.astype(jnp.bfloat16)
                pieces = [
                    half if q == p else jnp.zeros_like(half) for q in range(pair_count)
                ]
                rows.append(jnp.concatenate(pieces, axis=1))
        added = jnp.dot(
            jnp.concatenate(rows, axis=0), values, preferred_element_type=jnp.float32
        )
        for k in range(group_pages):
            sum_scr[owners[k]] += added[k * heads : (k + 1) * heads]
        return carry

    lax.fori_loop(0, groups, sum_group, 0, unroll=2)

    lane = lax.broadcasted_iota(jnp.int32, (heads, 128), 1)
    stats = jnp.full((heads, 128), masked_score, jnp.float32)
    for r in range(requests):
        total = jnp.sum(total_scr[r], axis=1, keepdims=True)
        present = total > 0.0
        safe = jnp.where(present, total, 1.0)
        mean = (sum_scr[r] * (1.0 / safe)).astype(jnp.bfloat16)
        level = jnp.where(present, max_scr[r][:, :1] + jnp.log(safe), masked_score)
        stats = jnp.where(lane == r, level, stats)
        for b in range(blocks):
            out_ref[place_ref[b], r] = mean[b * heads_here : (b + 1) * heads_here]
    for b in range(blocks):
        stat_ref[place_ref[b]] = stats[b * heads_here : (b + 1) * heads_here]


def attend(query_full, latent_cache, page_owner, places, score_scale, latent_size):
    requests, heads, entry_size = query_full.shape
    pages, page_len, _ = latent_cache.shape
    blocks = places.shape[0]
    heads_here = heads // blocks
    group_pages = 4
    vmem = pl.BlockSpec(memory_space=pltpu.VMEM)
    smem = pl.BlockSpec(memory_space=pltpu.SMEM)
    pair_len = 2 * page_len
    return pl.pallas_call(
        functools.partial(attend_kernel, score_scale, group_pages),
        out_shape=(
            jax.ShapeDtypeStruct((blocks, requests, heads_here, latent_size), jnp.bfloat16),
            jax.ShapeDtypeStruct((blocks, heads_here, 128), jnp.float32),
        ),
        in_specs=[smem, smem, vmem, vmem],
        out_specs=(vmem, vmem),
        scratch_shapes=[
            pltpu.VMEM((pages // 2, heads, pair_len), jnp.float32),
            pltpu.VMEM((requests + 1, heads, pair_len), jnp.float32),
            pltpu.VMEM((requests + 1, heads, pair_len), jnp.float32),
            pltpu.VMEM((requests + 1, heads, latent_size), jnp.float32),
        ],
        compiler_params=pltpu.CompilerParams(vmem_limit_bytes=VMEM_LIMIT),
        cost_estimate=pl.CostEstimate(
            flops=2 * pages * page_len * heads * (entry_size + latent_size) * 4,
            bytes_accessed=pages * page_len * entry_size * 2,
            transcendentals=pages * page_len * heads,
        ),
        name="attend",
    )(page_owner, places, query_full, pltpu.with_memory_space_constraint(latent_cache, pltpu.VMEM))


VMEM_LIMIT = 40 * 1024 * 1024


def body(query_nope, query_rope, key_absorb, value_absorb, output_weight, latent_cache, page_owner, ring):
    requests, heads_here, nope_size = query_nope.shape
    latent_size = key_absorb.shape[2]
    rope_size = query_rope.shape[1] // heads_here
    score_scale = (nope_size + rope_size) ** (-0.5)
    count = len(ring)
    query_latent = jnp.einsum(
        "rhn,hnl->rhl", query_nope, key_absorb, preferred_element_type=jnp.float32
    ).astype(jnp.bfloat16)
    own = jnp.concatenate(
        [query_latent, query_rope.reshape(requests, heads_here, rope_size)], axis=2
    )

    after = [(ring[i], ring[(i + 1) % count]) for i in range(count)]
    before = [(b, a) for a, b in after]
    blocks, offsets = [own], [0]
    forward = backward = own
    for step in range(1, count // 2 + 1):
        forward = lax.ppermute(forward, "ctx", after)
        blocks.append(forward)
        offsets.append(-step)
        if 2 * step < count:
            backward = lax.ppermute(backward, "ctx", before)
            blocks.append(backward)
            offsets.append(step)
    query_full = jnp.concatenate(blocks, axis=1)

    position = jnp.array([ring.index(i) for i in range(count)], jnp.int32)[lax.axis_index("ctx")]
    places = jnp.array(ring, jnp.int32)[
        (position + jnp.array(offsets, jnp.int32) + count) % count
    ]
    mean, stats = attend(query_full, latent_cache, page_owner, places, score_scale, latent_size)

    got_stats = lax.all_to_all(stats, "ctx", split_axis=0, concat_axis=0, tiled=True)
    got_mean = lax.all_to_all(mean, "ctx", split_axis=0, concat_axis=0, tiled=True)
    level = got_stats[:, :, :requests]
    share = jnp.exp(level - jnp.max(level, axis=0, keepdims=True))
    share = share / jnp.sum(share, axis=0, keepdims=True)
    attended = jnp.sum(
        share.transpose(0, 2, 1)[..., None] * got_mean.astype(jnp.float32), axis=0
    ).astype(jnp.bfloat16)
    head_out = jnp.einsum(
        "rhl,hlv->rhv", attended, value_absorb, preferred_element_type=jnp.float32
    ).astype(jnp.bfloat16)
    partial_out = jnp.dot(
        head_out.reshape(requests, -1), output_weight, preferred_element_type=jnp.float32
    ).astype(jnp.bfloat16)
    owners = lax.axis_size(("ctx", "head"))
    pieces = partial_out.reshape(requests, owners, -1).transpose(1, 0, 2)
    pieces = lax.all_to_all(pieces, ("ctx", "head"), split_axis=0, concat_axis=0, tiled=True)
    return jnp.sum(pieces.astype(jnp.float32), axis=0).astype(jnp.bfloat16)


def solution(mesh):
    return jax.shard_map(
        functools.partial(body, ring=ring_order(mesh.shape["ctx"])),
        mesh=mesh,
        in_specs=(
            P("groups", ("ctx", "head"), None),
            P("groups", ("ctx", "head")),
            P(("ctx", "head"), None, None),
            P(("ctx", "head"), None, None),
            P(("ctx", "head"), None),
            P(("groups", "ctx"), None, None),
            P(("groups", "ctx")),
        ),
        out_specs=P("groups", ("ctx", "head")),
        check_vma=False,
    )
```

```python
import functools

import jax
import jax.numpy as jnp
from jax import lax
from jax.experimental import pallas as pl
from jax.experimental.pallas import tpu as pltpu
from jax.sharding import PartitionSpec as P

masked_score = -1e30
LANES = 128
GROUP_PAGES = 4
MIB = 1024 * 1024

VMEM_SPEC = pl.BlockSpec(memory_space=pltpu.VMEM)
SMEM_SPEC = pl.BlockSpec(memory_space=pltpu.SMEM)


def in_vmem(x):
    return pltpu.with_memory_space_constraint(x, pltpu.VMEM)


def ring_order(count):
    if count % 2:
        return list(range(count))
    return list(range(0, count, 2)) + list(range(count - 1, 0, -2))


def split_level(level):
    high = level.astype(jnp.bfloat16)
    rest = level - high.astype(jnp.float32)
    middle = rest.astype(jnp.bfloat16)
    low = (rest - middle.astype(jnp.float32)).astype(jnp.bfloat16)
    return high, middle, low


def store_level(message_ref, row, level):
    for i, part in enumerate(split_level(level)):
        message_ref[row, :, i * LANES : (i + 1) * LANES] = part


def load_level(message_ref, row):
    parts = [
        message_ref[row, :, i * LANES : (i + 1) * LANES].astype(jnp.float32) for i in range(3)
    ]
    return (parts[0] + parts[1]) + parts[2]


def attend_kernel(score_scale, chunks, blocks, owner_ref, query_ref, cache_ref, weight_ref, *refs):
    message_refs = refs[:blocks]
    (
        weight_out, cache_scr, score_scr, max_scr, total_scr, sum_scr, cache_sem, weight_sem
    ) = refs[blocks:]
    requests, heads, entry_size = query_ref.shape
    pages, page_len, _ = cache_ref.shape
    _, heads_here, latent_size = message_refs[0].shape
    pair_len = 2 * page_len
    pair_count = GROUP_PAGES // 2
    groups_chunk = pages // GROUP_PAGES // chunks
    pages_chunk = pages // chunks
    group_len = GROUP_PAGES * page_len

    def cache_copy(c):
        rows = pl.ds(c * pages_chunk, pages_chunk)
        return pltpu.make_async_copy(cache_ref.at[rows], cache_scr.at[rows], cache_sem.at[c])

    for c in range(chunks):
        cache_copy(c).start()
    weight_copy = pltpu.make_async_copy(weight_ref, weight_out, weight_sem)
    weight_copy.start()

    first_half = lax.broadcasted_iota(jnp.int32, (heads, pair_len), 1) < page_len

    for r in range(requests + 1):
        max_scr[r] = jnp.full((heads, pair_len), masked_score, jnp.float32)
        total_scr[r] = jnp.zeros((heads, pair_len), jnp.float32)
        sum_scr[r] = jnp.zeros((heads, latent_size), jnp.float32)

    def owners_of(g):
        raw = [owner_ref[g * GROUP_PAGES + k] for k in range(GROUP_PAGES)]
        return [jnp.where(o < 0, requests, o) for o in raw]

    def score_group(g):
        owners = owners_of(g)
        keys = cache_scr[pl.ds(g * GROUP_PAGES, GROUP_PAGES)].reshape(group_len, entry_size)
        queries = jnp.concatenate(
            [query_ref[jnp.minimum(o, requests - 1)] for o in owners], axis=0
        )
        scores = lax.dot_general(
            queries, keys, (((1,), (1,)), ((), ())), preferred_element_type=jnp.float32
        )
        for p in range(pair_count):
            left, right = 2 * p, 2 * p + 1
            columns = slice(p * pair_len, (p + 1) * pair_len)
            pair = score_scale * jnp.where(
                first_half,
                scores[left * heads : (left + 1) * heads, columns],
                scores[right * heads : (right + 1) * heads, columns],
            )
            score_scr[g * pair_count + p] = pair
            max_scr[owners[left]] = jnp.maximum(
                max_scr[owners[left]], jnp.where(first_half, pair, masked_score)
            )
            max_scr[owners[right]] = jnp.maximum(
                max_scr[owners[right]], jnp.where(first_half, masked_score, pair)
            )

    def score_chunk(c, carry):
        cache_copy(c).wait()
        for i in range(groups_chunk):
            score_group(c * groups_chunk + i)
        return carry

    lax.fori_loop(0, chunks, score_chunk, 0)

    for r in range(requests + 1):
        top = jnp.max(max_scr[r], axis=1, keepdims=True)
        max_scr[r] = jnp.broadcast_to(top, (heads, pair_len))

    def sum_group(g):
        owners = owners_of(g)
        values = cache_scr[pl.ds(g * GROUP_PAGES, GROUP_PAGES)].reshape(group_len, entry_size)[
            :, :latent_size
        ]
        rows = []
        for p in range(pair_count):
            left, right = owners[2 * p], owners[2 * p + 1]
            offset = jnp.where(first_half, max_scr[left], max_scr[right])
            weight = jnp.exp(score_scr[g * pair_count + p] - offset)
            left_weight = jnp.where(first_half, weight, 0.0)
            right_weight = jnp.where(first_half, 0.0, weight)
            total_scr[left] += left_weight
            total_scr[right] += right_weight
            for part in (left_weight, right_weight):
                half = part.astype(jnp.bfloat16)
                pieces = [half if q == p else jnp.zeros_like(half) for q in range(pair_count)]
                rows.append(jnp.concatenate(pieces, axis=1))
        added = jnp.dot(
            jnp.concatenate(rows, axis=0), values, preferred_element_type=jnp.float32
        )
        for k in range(GROUP_PAGES):
            sum_scr[owners[k]] += added[k * heads : (k + 1) * heads]

    def sum_chunk(c, carry):
        for i in range(groups_chunk):
            sum_group(c * groups_chunk + i)
        return carry

    lax.fori_loop(0, chunks, sum_chunk, 0)

    lane = lax.broadcasted_iota(jnp.int32, (heads, LANES), 1)
    stats = jnp.full((heads, LANES), masked_score, jnp.float32)
    for r in range(requests):
        total = jnp.sum(total_scr[r], axis=1, keepdims=True)
        present = total > 0.0
        safe = jnp.where(present, total, 1.0)
        mean = (sum_scr[r] * (1.0 / safe)).astype(jnp.bfloat16)
        level = jnp.where(present, max_scr[r][:, :1] + jnp.log(safe), masked_score)
        stats = jnp.where(lane == r, level, stats)
        for b in range(blocks):
            message_refs[b][r] = mean[b * heads_here : (b + 1) * heads_here]
    for b in range(blocks):
        message_refs[b][requests] = jnp.zeros((heads_here, latent_size), jnp.bfloat16)
        store_level(message_refs[b], requests, stats[b * heads_here : (b + 1) * heads_here])
    weight_copy.wait()


def attend(query_full, latent_cache, page_owner, output_weight, score_scale, latent_size, blocks):
    requests, heads, entry_size = query_full.shape
    pages, page_len, _ = latent_cache.shape
    heads_here = heads // blocks
    pair_len = 2 * page_len
    groups = pages // GROUP_PAGES
    chunks = groups // max(d for d in range(1, 9) if groups % d == 0)
    any_spec = pl.BlockSpec(memory_space=pl.ANY)
    out = pl.pallas_call(
        functools.partial(attend_kernel, score_scale, chunks, blocks),
        out_shape=[
            pltpu.VMEM((requests + 1, heads_here, latent_size), jnp.bfloat16)
            for _ in range(blocks)
        ]
        + [pltpu.VMEM(output_weight.shape, output_weight.dtype)],
        in_specs=[SMEM_SPEC, VMEM_SPEC, any_spec, any_spec],
        out_specs=[VMEM_SPEC] * (blocks + 1),
        scratch_shapes=[
            pltpu.VMEM(latent_cache.shape, latent_cache.dtype),
            pltpu.VMEM((pages // 2, heads, pair_len), jnp.float32),
            pltpu.VMEM((requests + 1, heads, pair_len), jnp.float32),
            pltpu.VMEM((requests + 1, heads, pair_len), jnp.float32),
            pltpu.VMEM((requests + 1, heads, latent_size), jnp.float32),
            pltpu.SemaphoreType.DMA((chunks,)),
            pltpu.SemaphoreType.DMA,
        ],
        compiler_params=pltpu.CompilerParams(vmem_limit_bytes=34 * MIB),
        cost_estimate=pl.CostEstimate(
            flops=2 * pages * page_len * heads * (entry_size + latent_size) * 4,
            bytes_accessed=pages * page_len * entry_size * 2,
            transcendentals=pages * page_len * heads,
        ),
        name="attend",
    )(page_owner, in_vmem(query_full), latent_cache, output_weight)
    return out[:blocks], out[blocks]


def shares(levels):
    top = functools.reduce(jnp.maximum, levels)
    parts = [jnp.exp(level - top) for level in levels]
    total = functools.reduce(jnp.add, parts)
    return [part / total for part in parts], top + jnp.log(total)


def merge_kernel(own_ref, got_ref, out_ref):
    requests = own_ref.shape[0] - 1
    both = (own_ref, got_ref)
    weights, level = shares([load_level(ref, requests) for ref in both])
    for r in range(requests):
        out_ref[r] = sum(
            w[:, r : r + 1] * ref[r].astype(jnp.float32) for w, ref in zip(weights, both)
        ).astype(jnp.bfloat16)
    out_ref[requests] = jnp.zeros(out_ref.shape[1:], jnp.bfloat16)
    store_level(out_ref, requests, level)


def merge(own, got):
    return pl.pallas_call(
        merge_kernel,
        out_shape=pltpu.VMEM(own.shape, own.dtype),
        in_specs=[VMEM_SPEC] * 2,
        out_specs=VMEM_SPEC,
        cost_estimate=pl.CostEstimate(flops=4 * own.size, bytes_accessed=0, transcendentals=0),
        name="merge",
    )(in_vmem(own), in_vmem(got))


def finish_kernel(
    block_columns, here_ref, own_ref, forward_ref, backward_ref, value_ref, weight_ref, out_ref,
    attended_scr, head_scr,
):
    requests, heads_here = own_ref.shape[0] - 1, own_ref.shape[1]
    value_size = value_ref.shape[2]
    owners, _, width = out_ref.shape
    messages = (own_ref, forward_ref, backward_ref)
    weights, _ = shares([load_level(ref, requests) for ref in messages])
    for r in range(requests):
        attended_scr[r * heads_here : (r + 1) * heads_here] = sum(
            w[:, r : r + 1] * ref[r].astype(jnp.float32) for w, ref in zip(weights, messages)
        )
    attended = attended_scr[...].astype(jnp.bfloat16)
    row = lax.broadcasted_iota(jnp.int32, (requests, requests * heads_here), 0)
    column = lax.broadcasted_iota(jnp.int32, (requests, requests * heads_here), 1)
    for h in range(heads_here):
        pick = jnp.where(column == row * heads_here + h, 1.0, 0.0).astype(jnp.bfloat16)
        rows = jnp.dot(pick, attended, preferred_element_type=jnp.float32).astype(jnp.bfloat16)
        head_scr[:, h * value_size : (h + 1) * value_size] = jnp.dot(
            rows, value_ref[h], preferred_element_type=jnp.float32
        ).astype(jnp.bfloat16)
    head_out = head_scr[...]
    per_block = block_columns // width
    bits = owners.bit_length() - 1
    for j in range(owners // per_block):
        product = jnp.dot(
            head_out,
            weight_ref[:, j * block_columns : (j + 1) * block_columns],
            preferred_element_type=jnp.float32,
        ).astype(jnp.bfloat16)
        for i in range(per_block):
            distance = here_ref[0] ^ (j * per_block + i)
            place = sum(((distance >> b) & 1) << (bits - 1 - b) for b in range(bits))
            out_ref[place] = product[:, i * width : (i + 1) * width]


def finish(here, own, forward, backward, value_absorb, weight, owners):
    requests, heads_here = own.shape[0] - 1, own.shape[1]
    latent_size, value_size = value_absorb.shape[1:]
    depth, columns = weight.shape
    width = columns // owners
    block_columns = width
    while block_columns % LANES:
        block_columns *= 2
    return pl.pallas_call(
        functools.partial(finish_kernel, block_columns),
        out_shape=pltpu.VMEM((owners, requests, width), jnp.bfloat16),
        in_specs=[SMEM_SPEC] + [VMEM_SPEC] * 5,
        out_specs=VMEM_SPEC,
        scratch_shapes=[
            pltpu.VMEM((requests * heads_here, latent_size), jnp.float32),
            pltpu.VMEM((requests, heads_here * value_size), jnp.bfloat16),
        ],
        compiler_params=pltpu.CompilerParams(vmem_limit_bytes=8 * MIB),
        cost_estimate=pl.CostEstimate(
            flops=2 * 256 * depth * columns, bytes_accessed=0, transcendentals=0
        ),
        name="finish",
    )(here, *[in_vmem(x) for x in (own, forward, backward, value_absorb, weight)])


def body(
    query_nope, query_rope, key_absorb, value_absorb, output_weight, latent_cache, page_owner, ring
):
    requests, heads_here, nope_size = query_nope.shape
    latent_size = key_absorb.shape[2]
    rope_size = query_rope.shape[1] // heads_here
    score_scale = (nope_size + rope_size) ** (-0.5)
    count = len(ring)
    query_latent = jnp.einsum(
        "rhn,hnl->rhl", query_nope, key_absorb, preferred_element_type=jnp.float32
    ).astype(jnp.bfloat16)
    own = jnp.concatenate(
        [query_latent, query_rope.reshape(requests, heads_here, rope_size)], axis=2
    )

    after = [(ring[i], ring[(i + 1) % count]) for i in range(count)]
    before = [(b, a) for a, b in after]
    blocks, offsets = [own], [0]
    forward = backward = own
    for step in range(1, count // 2 + 1):
        forward = lax.ppermute(forward, "ctx", after)
        blocks.append(forward)
        offsets.append(-step)
        if 2 * step < count:
            backward = lax.ppermute(backward, "ctx", before)
            blocks.append(backward)
            offsets.append(step)
    query_full = jnp.concatenate(blocks, axis=1)

    messages, weight = attend(
        query_full, latent_cache, page_owner, output_weight, score_scale, latent_size, count
    )
    message_to = {offset % count: message for offset, message in zip(offsets, messages)}

    forward_steps, backward_steps = count // 2, (count - 1) // 2
    forward, backward = message_to[forward_steps], message_to[-backward_steps % count]
    for step in range(1, forward_steps + 1):
        forward = lax.ppermute(forward, "ctx", after)
        if step <= backward_steps:
            backward = lax.ppermute(backward, "ctx", before)
        if step < forward_steps:
            forward = merge(message_to[forward_steps - step], forward)
        if step < backward_steps:
            backward = merge(message_to[(step - backward_steps) % count], backward)

    axes = ("ctx", "head")
    owners = lax.axis_size(axes)
    here = lax.axis_index(axes).astype(jnp.int32).reshape(1)
    pieces = finish(here, message_to[0], forward, backward, value_absorb, weight, owners)
    distance = 1
    while distance < owners:
        pairs = [(i, i ^ distance) for i in range(owners)]
        half = pieces.shape[0] // 2
        got = lax.ppermute(pieces[half:], axes, pairs)
        pieces = (pieces[:half].astype(jnp.float32) + got.astype(jnp.float32)).astype(
            jnp.bfloat16
        )
        distance *= 2
    return pieces[0]


def solution(mesh):
    return jax.shard_map(
        functools.partial(body, ring=ring_order(mesh.shape["ctx"])),
        mesh=mesh,
        in_specs=(
            P("groups", ("ctx", "head"), None),
            P("groups", ("ctx", "head")),
            P(("ctx", "head"), None, None),
            P(("ctx", "head"), None, None),
            P(("ctx", "head"), None),
            P(("groups", "ctx"), None, None),
            P(("groups", "ctx")),
        ),
        out_specs=P("groups", ("ctx", "head")),
        check_vma=False,
    )
```

```python
import functools

import jax
import jax.numpy as jnp
from jax import lax
from jax.experimental import pallas as pl
from jax.experimental.pallas import tpu as pltpu
from jax.sharding import PartitionSpec as P

masked_score = -1e30
LANES = 128
GROUP_PAGES = 4
MIB = 1024 * 1024

VMEM_SPEC = pl.BlockSpec(memory_space=pltpu.VMEM)
SMEM_SPEC = pl.BlockSpec(memory_space=pltpu.SMEM)


def in_vmem(x):
    return pltpu.with_memory_space_constraint(x, pltpu.VMEM)


def ring_order(count):
    if count % 2:
        return list(range(count))
    return list(range(0, count, 2)) + list(range(count - 1, 0, -2))


def split_level(level):
    high = level.astype(jnp.bfloat16)
    rest = level - high.astype(jnp.float32)
    middle = rest.astype(jnp.bfloat16)
    low = (rest - middle.astype(jnp.float32)).astype(jnp.bfloat16)
    return high, middle, low


def store_level(message_ref, row, level):
    for i, part in enumerate(split_level(level)):
        message_ref[row, :, i * LANES : (i + 1) * LANES] = part


def load_level(message_ref, row):
    parts = [
        message_ref[row, :, i * LANES : (i + 1) * LANES].astype(jnp.float32) for i in range(3)
    ]
    return (parts[0] + parts[1]) + parts[2]


def attend_kernel(score_scale, chunks, parts, owner_ref, query_ref, cache_ref, weight_ref, *refs):
    message_refs = refs[: len(parts)]
    (
        weight_out, cache_scr, score_scr, max_scr, total_scr, sum_scr, cache_sem, weight_sem
    ) = refs[len(parts) :]
    requests, heads, entry_size = query_ref.shape
    pages, page_len, _ = cache_ref.shape
    _, heads_here, latent_size = message_refs[0].shape
    pair_len = 2 * page_len
    pair_count = GROUP_PAGES // 2
    groups_chunk = pages // GROUP_PAGES // chunks
    pages_chunk = pages // chunks
    group_len = GROUP_PAGES * page_len

    def cache_copy(c):
        rows = pl.ds(c * pages_chunk, pages_chunk)
        return pltpu.make_async_copy(cache_ref.at[rows], cache_scr.at[rows], cache_sem.at[c])

    for c in range(chunks):
        cache_copy(c).start()
    weight_copy = pltpu.make_async_copy(weight_ref, weight_out, weight_sem)
    weight_copy.start()

    first_half = lax.broadcasted_iota(jnp.int32, (heads, pair_len), 1) < page_len

    for r in range(requests + 1):
        max_scr[r] = jnp.full((heads, pair_len), masked_score, jnp.float32)
        total_scr[r] = jnp.zeros((heads, pair_len), jnp.float32)
        sum_scr[r] = jnp.zeros((heads, latent_size), jnp.float32)

    def owners_of(g):
        raw = [owner_ref[g * GROUP_PAGES + k] for k in range(GROUP_PAGES)]
        return [jnp.where(o < 0, requests, o) for o in raw]

    def score_group(g):
        owners = owners_of(g)
        keys = cache_scr[pl.ds(g * GROUP_PAGES, GROUP_PAGES)].reshape(group_len, entry_size)
        queries = jnp.concatenate(
            [query_ref[jnp.minimum(o, requests - 1)] for o in owners], axis=0
        )
        scores = lax.dot_general(
            queries, keys, (((1,), (1,)), ((), ())), preferred_element_type=jnp.float32
        )
        for p in range(pair_count):
            left, right = 2 * p, 2 * p + 1
            columns = slice(p * pair_len, (p + 1) * pair_len)
            pair = score_scale * jnp.where(
                first_half,
                scores[left * heads : (left + 1) * heads, columns],
                scores[right * heads : (right + 1) * heads, columns],
            )
            score_scr[g * pair_count + p] = pair
            max_scr[owners[left]] = jnp.maximum(
                max_scr[owners[left]], jnp.where(first_half, pair, masked_score)
            )
            max_scr[owners[right]] = jnp.maximum(
                max_scr[owners[right]], jnp.where(first_half, masked_score, pair)
            )

    def score_chunk(c, carry):
        cache_copy(c).wait()
        for i in range(groups_chunk):
            score_group(c * groups_chunk + i)
        return carry

    lax.fori_loop(0, chunks, score_chunk, 0)

    for r in range(requests + 1):
        top = jnp.max(max_scr[r], axis=1, keepdims=True)
        max_scr[r] = jnp.broadcast_to(top, (heads, pair_len))

    def sum_group(g):
        owners = owners_of(g)
        values = cache_scr[pl.ds(g * GROUP_PAGES, GROUP_PAGES)].reshape(group_len, entry_size)[
            :, :latent_size
        ]
        rows = []
        for p in range(pair_count):
            left, right = owners[2 * p], owners[2 * p + 1]
            offset = jnp.where(first_half, max_scr[left], max_scr[right])
            weight = jnp.exp(score_scr[g * pair_count + p] - offset)
            left_weight = jnp.where(first_half, weight, 0.0)
            right_weight = jnp.where(first_half, 0.0, weight)
            total_scr[left] += left_weight
            total_scr[right] += right_weight
            for part in (left_weight, right_weight):
                half = part.astype(jnp.bfloat16)
                pieces = [half if q == p else jnp.zeros_like(half) for q in range(pair_count)]
                rows.append(jnp.concatenate(pieces, axis=1))
        added = jnp.dot(
            jnp.concatenate(rows, axis=0), values, preferred_element_type=jnp.float32
        )
        for k in range(GROUP_PAGES):
            sum_scr[owners[k]] += added[k * heads : (k + 1) * heads]

    def sum_chunk(c, carry):
        for i in range(groups_chunk):
            sum_group(c * groups_chunk + i)
        return carry

    lax.fori_loop(0, chunks, sum_chunk, 0)

    lane = lax.broadcasted_iota(jnp.int32, (heads, LANES), 1)
    stats = jnp.full((heads, LANES), masked_score, jnp.float32)
    for r in range(requests):
        total = jnp.sum(total_scr[r], axis=1, keepdims=True)
        present = total > 0.0
        safe = jnp.where(present, total, 1.0)
        mean = (sum_scr[r] * (1.0 / safe)).astype(jnp.bfloat16)
        level = jnp.where(present, max_scr[r][:, :1] + jnp.log(safe), masked_score)
        stats = jnp.where(lane == r, level, stats)
        for ref, (block, low, high) in zip(message_refs, parts):
            if low <= r < high:
                ref[r - low] = mean[block * heads_here : (block + 1) * heads_here]
    for ref, (block, low, high) in zip(message_refs, parts):
        ref[high - low] = jnp.zeros((heads_here, latent_size), jnp.bfloat16)
        level = jnp.where((lane >= low) & (lane < high), stats, masked_score)
        store_level(ref, high - low, level[block * heads_here : (block + 1) * heads_here])
    weight_copy.wait()


def attend(query_full, latent_cache, page_owner, output_weight, score_scale, latent_size, blocks, parts):
    requests, heads, entry_size = query_full.shape
    pages, page_len, _ = latent_cache.shape
    heads_here = heads // blocks
    pair_len = 2 * page_len
    groups = pages // GROUP_PAGES
    chunks = groups // max(d for d in range(1, 15) if groups % d == 0)
    any_spec = pl.BlockSpec(memory_space=pl.ANY)
    out = pl.pallas_call(
        functools.partial(attend_kernel, score_scale, chunks, parts),
        out_shape=[
            pltpu.VMEM((high - low + 1, heads_here, latent_size), jnp.bfloat16)
            for _, low, high in parts
        ]
        + [pltpu.VMEM(output_weight.shape, output_weight.dtype)],
        in_specs=[SMEM_SPEC, VMEM_SPEC, any_spec, any_spec],
        out_specs=[VMEM_SPEC] * (len(parts) + 1),
        scratch_shapes=[
            pltpu.VMEM(latent_cache.shape, latent_cache.dtype),
            pltpu.VMEM((pages // 2, heads, pair_len), jnp.float32),
            pltpu.VMEM((requests + 1, heads, pair_len), jnp.float32),
            pltpu.VMEM((requests + 1, heads, pair_len), jnp.float32),
            pltpu.VMEM((requests + 1, heads, latent_size), jnp.float32),
            pltpu.SemaphoreType.DMA((chunks,)),
            pltpu.SemaphoreType.DMA,
        ],
        compiler_params=pltpu.CompilerParams(vmem_limit_bytes=34 * MIB),
        cost_estimate=pl.CostEstimate(
            flops=2 * pages * page_len * heads * (entry_size + latent_size) * 4,
            bytes_accessed=pages * page_len * entry_size * 2,
            transcendentals=pages * page_len * heads,
        ),
        name="attend",
    )(page_owner, in_vmem(query_full), latent_cache, output_weight)
    return out[:-1], out[-1]


def shares(levels):
    top = functools.reduce(jnp.maximum, levels)
    parts = [jnp.exp(level - top) for level in levels]
    total = functools.reduce(jnp.add, parts)
    return [part / total for part in parts], top + jnp.log(total)


def merge_kernel(first, own_ref, got_ref, out_ref):
    requests, got_rows = own_ref.shape[0] - 1, got_ref.shape[0] - 1
    weights, level = shares([load_level(own_ref, requests), load_level(got_ref, got_rows)])
    for r in range(requests):
        if not 0 <= r - first < got_rows:
            out_ref[r] = own_ref[r]
            continue
        out_ref[r] = sum(
            w[:, r : r + 1] * rows.astype(jnp.float32)
            for w, rows in zip(weights, (own_ref[r], got_ref[r - first]))
        ).astype(jnp.bfloat16)
    out_ref[requests] = jnp.zeros(out_ref.shape[1:], jnp.bfloat16)
    store_level(out_ref, requests, level)


def merge(own, got, first=0):
    return pl.pallas_call(
        functools.partial(merge_kernel, first),
        out_shape=pltpu.VMEM(own.shape, own.dtype),
        in_specs=[VMEM_SPEC] * 2,
        out_specs=VMEM_SPEC,
        compiler_params=pltpu.CompilerParams(vmem_limit_bytes=2 * MIB),
        cost_estimate=pl.CostEstimate(flops=4 * own.size, bytes_accessed=0, transcendentals=0),
        name="merge",
    )(in_vmem(own), in_vmem(got))


def finish_kernel(
    block_columns, radices, here_ref, own_ref, forward_ref, backward_ref, value_ref, weight_ref, out_ref,
    attended_scr, head_scr,
):
    requests, heads_here = own_ref.shape[0] - 1, own_ref.shape[1]
    value_size = value_ref.shape[2]
    owners, _, width = out_ref.shape
    messages = (own_ref, forward_ref, backward_ref)
    weights, _ = shares([load_level(ref, requests) for ref in messages])
    for r in range(requests):
        attended_scr[r * heads_here : (r + 1) * heads_here] = sum(
            w[:, r : r + 1] * ref[r].astype(jnp.float32) for w, ref in zip(weights, messages)
        )
    attended = attended_scr[...].astype(jnp.bfloat16)
    row = lax.broadcasted_iota(jnp.int32, (requests, requests * heads_here), 0)
    column = lax.broadcasted_iota(jnp.int32, (requests, requests * heads_here), 1)
    for h in range(heads_here):
        pick = jnp.where(column == row * heads_here + h, 1.0, 0.0).astype(jnp.bfloat16)
        rows = jnp.dot(pick, attended, preferred_element_type=jnp.float32).astype(jnp.bfloat16)
        head_scr[:, h * value_size : (h + 1) * value_size] = jnp.dot(
            rows, value_ref[h], preferred_element_type=jnp.float32
        ).astype(jnp.bfloat16)
    head_out = head_scr[...]
    per_block = block_columns // width
    for j in range(owners // per_block):
        product = jnp.dot(
            head_out,
            weight_ref[:, j * block_columns : (j + 1) * block_columns],
            preferred_element_type=jnp.float32,
        ).astype(jnp.bfloat16)
        for i in range(per_block):
            distance = here_ref[0] ^ (j * per_block + i)
            place = 0
            for radix in radices:
                place = place * radix + (distance & (radix - 1))
                distance = distance >> (radix.bit_length() - 1)
            out_ref[place] = product[:, i * width : (i + 1) * width]


def finish(here, own, forward, backward, value_absorb, weight, radices):
    requests, heads_here = own.shape[0] - 1, own.shape[1]
    latent_size, value_size = value_absorb.shape[1:]
    depth, columns = weight.shape
    owners = functools.reduce(lambda a, b: a * b, radices)
    width = columns // owners
    block_columns = width
    while block_columns % LANES:
        block_columns *= 2
    return pl.pallas_call(
        functools.partial(finish_kernel, block_columns, radices),
        out_shape=pltpu.VMEM((owners, requests, width), jnp.bfloat16),
        in_specs=[SMEM_SPEC] + [VMEM_SPEC] * 5,
        out_specs=VMEM_SPEC,
        scratch_shapes=[
            pltpu.VMEM((requests * heads_here, latent_size), jnp.float32),
            pltpu.VMEM((requests, heads_here * value_size), jnp.bfloat16),
        ],
        compiler_params=pltpu.CompilerParams(vmem_limit_bytes=8 * MIB),
        cost_estimate=pl.CostEstimate(
            flops=2 * 256 * depth * columns, bytes_accessed=0, transcendentals=0
        ),
        name="finish",
    )(here, *[in_vmem(x) for x in (own, forward, backward, value_absorb, weight)])


def body(
    query_nope, query_rope, key_absorb, value_absorb, output_weight, latent_cache, page_owner, ring
):
    requests, heads_here, nope_size = query_nope.shape
    latent_size = key_absorb.shape[2]
    rope_size = query_rope.shape[1] // heads_here
    score_scale = (nope_size + rope_size) ** (-0.5)
    count = len(ring)
    steps, half = count // 2, requests // 2
    query_latent = jnp.einsum(
        "rhn,hnl->rhl", query_nope, key_absorb, preferred_element_type=jnp.float32
    ).astype(jnp.bfloat16)
    own = jnp.concatenate(
        [query_latent, query_rope.reshape(-1, heads_here, latent_size)], axis=0
    )

    after = [(ring[i], ring[(i + 1) % count]) for i in range(count)]
    before = [(b, a) for a, b in after]
    middle = own.shape[0] // 2
    blocks, offsets = [own], [0]
    forward = backward = own
    for step in range(1, steps):
        forward = lax.ppermute(forward, "ctx", after)
        backward = lax.ppermute(backward, "ctx", before)
        blocks += [forward, backward]
        offsets += [-step, step]
    far = [
        lax.ppermute(forward[:middle], "ctx", after),
        lax.ppermute(backward[middle:], "ctx", before),
    ]
    blocks.append(jnp.concatenate(far, axis=0))
    offsets.append(steps)
    query_full = jnp.concatenate(
        [
            jnp.concatenate(
                [
                    block[:requests],
                    block[requests:].reshape(requests, heads_here, rope_size),
                ],
                axis=2,
            )
            for block in blocks
        ],
        axis=1,
    )

    parts = [(b, 0, requests) for b in range(count - 1)]
    parts += [(count - 1, 0, half), (count - 1, half, requests)]
    messages, weight = attend(
        query_full, latent_cache, page_owner, output_weight, score_scale, latent_size, count, parts
    )
    message_to = dict(zip(offsets[:-1], messages))

    forward, backward = messages[-2:]
    for step in range(1, steps + 1):
        forward = lax.ppermute(forward, "ctx", after)
        backward = lax.ppermute(backward, "ctx", before)
        if step < steps:
            forward = merge(message_to[steps - step], forward)
            backward = merge(message_to[step - steps], backward, half if step == 1 else 0)

    axes = ("ctx", "head")
    owners = lax.axis_size(axes)
    radices = []
    while functools.reduce(lambda a, b: a * b, radices, 1) < owners:
        left = owners // functools.reduce(lambda a, b: a * b, radices, 1)
        radices.append(4 if left % 4 == 0 else 2)
    here = lax.axis_index(axes).astype(jnp.int32).reshape(1)
    pieces = finish(here, message_to[0], forward, backward, value_absorb, weight, radices)
    unit = 1
    for radix in radices:
        share = pieces.shape[0] // radix
        got = [
            lax.ppermute(
                pieces[k * share : (k + 1) * share],
                axes,
                [(i, i ^ (k * unit)) for i in range(owners)],
            )
            for k in range(1, radix)
        ]
        pieces = sum(x.astype(jnp.float32) for x in [pieces[:share], *got]).astype(jnp.bfloat16)
        unit *= radix
    return pieces[0]


def solution(mesh):
    return jax.shard_map(
        functools.partial(body, ring=ring_order(mesh.shape["ctx"])),
        mesh=mesh,
        in_specs=(
            P("groups", ("ctx", "head"), None),
            P("groups", ("ctx", "head")),
            P(("ctx", "head"), None, None),
            P(("ctx", "head"), None, None),
            P(("ctx", "head"), None),
            P(("groups", "ctx"), None, None),
            P(("groups", "ctx")),
        ),
        out_specs=P("groups", ("ctx", "head")),
        check_vma=False,
    )
```

```python
import functools

import jax
import jax.numpy as jnp
from jax import lax
from jax.experimental import pallas as pl
from jax.experimental.pallas import tpu as pltpu
from jax.sharding import PartitionSpec as P

masked_score = -1e30
LANES = 128
GROUP_PAGES = 4
MIB = 1024 * 1024

VMEM_SPEC = pl.BlockSpec(memory_space=pltpu.VMEM)
SMEM_SPEC = pl.BlockSpec(memory_space=pltpu.SMEM)


def in_vmem(x):
    return pltpu.with_memory_space_constraint(x, pltpu.VMEM)


def split_level(level):
    high = level.astype(jnp.bfloat16)
    rest = level - high.astype(jnp.float32)
    middle = rest.astype(jnp.bfloat16)
    low = (rest - middle.astype(jnp.float32)).astype(jnp.bfloat16)
    return high, middle, low


def store_level(message_ref, row, level):
    for i, part in enumerate(split_level(level)):
        message_ref[row, :, i * LANES : (i + 1) * LANES] = part


def load_level(message_ref, row):
    parts = [
        message_ref[row, :, i * LANES : (i + 1) * LANES].astype(jnp.float32) for i in range(3)
    ]
    return (parts[0] + parts[1]) + parts[2]


def attend_kernel(score_scale, chunks, blocks, owner_ref, query_ref, cache_ref, weight_ref, *refs):
    message_refs = refs[:blocks]
    (
        weight_out, cache_scr, score_scr, max_scr, total_scr, sum_scr, cache_sem, weight_sem
    ) = refs[blocks:]
    requests, heads, entry_size = query_ref.shape
    pages, page_len, _ = cache_ref.shape
    _, heads_here, latent_size = message_refs[0].shape
    pair_len = 2 * page_len
    pair_count = GROUP_PAGES // 2
    groups_chunk = pages // GROUP_PAGES // chunks
    pages_chunk = pages // chunks
    group_len = GROUP_PAGES * page_len

    def cache_copy(c):
        rows = pl.ds(c * pages_chunk, pages_chunk)
        return pltpu.make_async_copy(cache_ref.at[rows], cache_scr.at[rows], cache_sem.at[c])

    for c in range(chunks):
        cache_copy(c).start()
    weight_copy = pltpu.make_async_copy(weight_ref, weight_out, weight_sem)
    weight_copy.start()

    first_half = lax.broadcasted_iota(jnp.int32, (heads, pair_len), 1) < page_len

    for r in range(requests + 1):
        max_scr[r] = jnp.full((heads, pair_len), masked_score, jnp.float32)
        total_scr[r] = jnp.zeros((heads, pair_len), jnp.float32)
        sum_scr[r] = jnp.zeros((heads, latent_size), jnp.float32)

    def owners_of(g):
        raw = [owner_ref[g * GROUP_PAGES + k] for k in range(GROUP_PAGES)]
        return [jnp.where(o < 0, requests, o) for o in raw]

    def score_group(g):
        owners = owners_of(g)
        keys = cache_scr[pl.ds(g * GROUP_PAGES, GROUP_PAGES)].reshape(group_len, entry_size)
        queries = jnp.concatenate(
            [query_ref[jnp.minimum(o, requests - 1)] for o in owners], axis=0
        )
        scores = lax.dot_general(
            queries, keys, (((1,), (1,)), ((), ())), preferred_element_type=jnp.float32
        )
        for p in range(pair_count):
            left, right = 2 * p, 2 * p + 1
            columns = slice(p * pair_len, (p + 1) * pair_len)
            pair = score_scale * jnp.where(
                first_half,
                scores[left * heads : (left + 1) * heads, columns],
                scores[right * heads : (right + 1) * heads, columns],
            )
            score_scr[g * pair_count + p] = pair
            max_scr[owners[left]] = jnp.maximum(
                max_scr[owners[left]], jnp.where(first_half, pair, masked_score)
            )
            max_scr[owners[right]] = jnp.maximum(
                max_scr[owners[right]], jnp.where(first_half, masked_score, pair)
            )

    def score_chunk(c, carry):
        cache_copy(c).wait()
        for i in range(groups_chunk):
            score_group(c * groups_chunk + i)
        return carry

    lax.fori_loop(0, chunks, score_chunk, 0)

    for r in range(requests + 1):
        top = jnp.max(max_scr[r], axis=1, keepdims=True)
        max_scr[r] = jnp.broadcast_to(top, (heads, pair_len))

    def sum_group(g):
        owners = owners_of(g)
        values = cache_scr[pl.ds(g * GROUP_PAGES, GROUP_PAGES)].reshape(group_len, entry_size)[
            :, :latent_size
        ]
        rows = []
        for p in range(pair_count):
            left, right = owners[2 * p], owners[2 * p + 1]
            offset = jnp.where(first_half, max_scr[left], max_scr[right])
            weight = jnp.exp(score_scr[g * pair_count + p] - offset)
            left_weight = jnp.where(first_half, weight, 0.0)
            right_weight = jnp.where(first_half, 0.0, weight)
            total_scr[left] += left_weight
            total_scr[right] += right_weight
            for part in (left_weight, right_weight):
                half = part.astype(jnp.bfloat16)
                pieces = [half if q == p else jnp.zeros_like(half) for q in range(pair_count)]
                rows.append(jnp.concatenate(pieces, axis=1))
        added = jnp.dot(
            jnp.concatenate(rows, axis=0), values, preferred_element_type=jnp.float32
        )
        for k in range(GROUP_PAGES):
            sum_scr[owners[k]] += added[k * heads : (k + 1) * heads]

    def sum_chunk(c, carry):
        for i in range(groups_chunk):
            sum_group(c * groups_chunk + i)
        return carry

    lax.fori_loop(0, chunks, sum_chunk, 0)

    lane = lax.broadcasted_iota(jnp.int32, (heads, LANES), 1)
    stats = jnp.full((heads, LANES), masked_score, jnp.float32)
    for r in range(requests):
        total = jnp.sum(total_scr[r], axis=1, keepdims=True)
        present = total > 0.0
        safe = jnp.where(present, total, 1.0)
        mean = (sum_scr[r] * (1.0 / safe)).astype(jnp.bfloat16)
        level = jnp.where(present, max_scr[r][:, :1] + jnp.log(safe), masked_score)
        stats = jnp.where(lane == r, level, stats)
        for b in range(blocks):
            message_refs[b][r] = mean[b * heads_here : (b + 1) * heads_here]
    for b in range(blocks):
        message_refs[b][requests] = jnp.zeros((heads_here, latent_size), jnp.bfloat16)
        store_level(message_refs[b], requests, stats[b * heads_here : (b + 1) * heads_here])
    weight_copy.wait()


def attend(query_full, latent_cache, page_owner, output_weight, score_scale, latent_size, blocks):
    requests, heads, entry_size = query_full.shape
    pages, page_len, _ = latent_cache.shape
    heads_here = heads // blocks
    pair_len = 2 * page_len
    groups = pages // GROUP_PAGES
    chunks = groups // max(d for d in range(1, 15) if groups % d == 0)
    any_spec = pl.BlockSpec(memory_space=pl.ANY)
    out = pl.pallas_call(
        functools.partial(attend_kernel, score_scale, chunks, blocks),
        out_shape=[
            pltpu.VMEM((requests + 1, heads_here, latent_size), jnp.bfloat16)
            for _ in range(blocks)
        ]
        + [pltpu.VMEM(output_weight.shape, output_weight.dtype)],
        in_specs=[SMEM_SPEC, VMEM_SPEC, any_spec, any_spec],
        out_specs=[VMEM_SPEC] * (blocks + 1),
        scratch_shapes=[
            pltpu.VMEM(latent_cache.shape, latent_cache.dtype),
            pltpu.VMEM((pages // 2, heads, pair_len), jnp.float32),
            pltpu.VMEM((requests + 1, heads, pair_len), jnp.float32),
            pltpu.VMEM((requests + 1, heads, pair_len), jnp.float32),
            pltpu.VMEM((requests + 1, heads, latent_size), jnp.float32),
            pltpu.SemaphoreType.DMA((chunks,)),
            pltpu.SemaphoreType.DMA,
        ],
        compiler_params=pltpu.CompilerParams(vmem_limit_bytes=34 * MIB),
        cost_estimate=pl.CostEstimate(
            flops=2 * pages * page_len * heads * (entry_size + latent_size) * 4,
            bytes_accessed=pages * page_len * entry_size * 2,
            transcendentals=pages * page_len * heads,
        ),
        name="attend",
    )(page_owner, in_vmem(query_full), latent_cache, output_weight)
    return out[:-1], out[-1]


def shares(levels):
    top = functools.reduce(jnp.maximum, levels)
    parts = [jnp.exp(level - top) for level in levels]
    total = functools.reduce(jnp.add, parts)
    return [part / total for part in parts], top + jnp.log(total)


def merge_kernel(own_ref, got_ref, out_ref):
    requests = own_ref.shape[0] - 1
    both = (own_ref, got_ref)
    weights, level = shares([load_level(ref, requests) for ref in both])
    for r in range(requests):
        out_ref[r] = sum(
            w[:, r : r + 1] * ref[r].astype(jnp.float32) for w, ref in zip(weights, both)
        ).astype(jnp.bfloat16)
    out_ref[requests] = jnp.zeros(out_ref.shape[1:], jnp.bfloat16)
    store_level(out_ref, requests, level)


def merge(own, got):
    return pl.pallas_call(
        merge_kernel,
        out_shape=pltpu.VMEM(own.shape, own.dtype),
        in_specs=[VMEM_SPEC] * 2,
        out_specs=VMEM_SPEC,
        compiler_params=pltpu.CompilerParams(vmem_limit_bytes=2 * MIB),
        cost_estimate=pl.CostEstimate(flops=4 * own.size, bytes_accessed=0, transcendentals=0),
        name="merge",
    )(in_vmem(own), in_vmem(got))


def finish_kernel(
    block_columns, radices, here_ref, value_ref, weight_ref, *refs
):
    messages, (out_ref, attended_scr, head_scr) = refs[:-3], refs[-3:]
    requests, heads_here = messages[0].shape[0] - 1, messages[0].shape[1]
    value_size = value_ref.shape[2]
    owners, _, width = out_ref.shape
    weights, _ = shares([load_level(ref, requests) for ref in messages])
    for r in range(requests):
        attended_scr[r * heads_here : (r + 1) * heads_here] = sum(
            w[:, r : r + 1] * ref[r].astype(jnp.float32) for w, ref in zip(weights, messages)
        )
    attended = attended_scr[...].astype(jnp.bfloat16)
    row = lax.broadcasted_iota(jnp.int32, (requests, requests * heads_here), 0)
    column = lax.broadcasted_iota(jnp.int32, (requests, requests * heads_here), 1)
    for h in range(heads_here):
        pick = jnp.where(column == row * heads_here + h, 1.0, 0.0).astype(jnp.bfloat16)
        rows = jnp.dot(pick, attended, preferred_element_type=jnp.float32).astype(jnp.bfloat16)
        head_scr[:, h * value_size : (h + 1) * value_size] = jnp.dot(
            rows, value_ref[h], preferred_element_type=jnp.float32
        ).astype(jnp.bfloat16)
    head_out = head_scr[...]
    per_block = block_columns // width
    for j in range(owners // per_block):
        product = jnp.dot(
            head_out,
            weight_ref[:, j * block_columns : (j + 1) * block_columns],
            preferred_element_type=jnp.float32,
        ).astype(jnp.bfloat16)
        for i in range(per_block):
            distance = here_ref[0] ^ (j * per_block + i)
            place = 0
            for radix in radices:
                place = place * radix + (distance & (radix - 1))
                distance = distance >> (radix.bit_length() - 1)
            out_ref[place] = product[:, i * width : (i + 1) * width]


def finish(here, messages, value_absorb, weight, radices):
    requests, heads_here = messages[0].shape[0] - 1, messages[0].shape[1]
    latent_size, value_size = value_absorb.shape[1:]
    depth, columns = weight.shape
    owners = functools.reduce(lambda a, b: a * b, radices)
    width = columns // owners
    block_columns = width
    while block_columns % LANES:
        block_columns *= 2
    return pl.pallas_call(
        functools.partial(finish_kernel, block_columns, radices),
        out_shape=pltpu.VMEM((owners, requests, width), jnp.bfloat16),
        in_specs=[SMEM_SPEC] + [VMEM_SPEC] * (2 + len(messages)),
        out_specs=VMEM_SPEC,
        scratch_shapes=[
            pltpu.VMEM((requests * heads_here, latent_size), jnp.float32),
            pltpu.VMEM((requests, heads_here * value_size), jnp.bfloat16),
        ],
        compiler_params=pltpu.CompilerParams(vmem_limit_bytes=8 * MIB),
        cost_estimate=pl.CostEstimate(
            flops=2 * 256 * depth * columns, bytes_accessed=0, transcendentals=0
        ),
        name="finish",
    )(here, *[in_vmem(x) for x in (value_absorb, weight, *messages)])


def body(
    query_nope, query_rope, key_absorb, value_absorb, output_weight, latent_cache, page_owner
):
    requests, heads_here, nope_size = query_nope.shape
    latent_size = key_absorb.shape[2]
    rope_size = query_rope.shape[1] // heads_here
    score_scale = (nope_size + rope_size) ** (-0.5)
    count = lax.axis_size("ctx")
    axes = ("ctx", "head")
    here = lax.axis_index(axes).astype(jnp.int32).reshape(1)

    def exchange(x, distance):
        return lax.ppermute(x, "ctx", [(i, i ^ distance) for i in range(count)])

    query_latent = jnp.einsum(
        "rhn,hnl->rhl", query_nope, key_absorb, preferred_element_type=jnp.float32
    ).astype(jnp.bfloat16)
    own = jnp.concatenate(
        [query_latent, query_rope.reshape(-1, heads_here, latent_size)], axis=0
    )
    own, here = lax.optimization_barrier((own, here))

    even = [*range(4, count, 2), 2] if count > 2 else []
    block_at = {0: own}
    for distance in even:
        block_at[distance] = exchange(own, distance)
    for distance in [0, *even]:
        block_at[distance ^ 1] = exchange(block_at[distance], 1)
    query_full = jnp.concatenate(
        [
            jnp.concatenate(
                [
                    block_at[d][:requests],
                    block_at[d][requests:].reshape(requests, heads_here, rope_size),
                ],
                axis=2,
            )
            for d in range(count)
        ],
        axis=1,
    )

    message_to, weight = attend(
        query_full, latent_cache, page_owner, output_weight, score_scale, latent_size, count
    )

    across = {distance: exchange(message_to[distance ^ 1], 1) for distance in [*even, 0]}
    arrived = [
        exchange(merge(message_to[distance], across[distance]), distance) for distance in even
    ]
    messages = [message_to[0], across[0], *arrived]

    owners = lax.axis_size(axes)
    radices = []
    while functools.reduce(lambda a, b: a * b, radices, 1) < owners:
        left = owners // functools.reduce(lambda a, b: a * b, radices, 1)
        radices.append(4 if left % 4 == 0 else 2)
    pieces = finish(here, messages, value_absorb, weight, radices)
    unit = 1
    for radix in radices:
        share = pieces.shape[0] // radix
        got = [
            lax.ppermute(
                pieces[k * share : (k + 1) * share],
                axes,
                [(i, i ^ (k * unit)) for i in range(owners)],
            )
            for k in range(1, radix)
        ]
        pieces = sum(x.astype(jnp.float32) for x in [pieces[:share], *got]).astype(jnp.bfloat16)
        unit *= radix
    return pieces[0]


def solution(mesh):
    return jax.shard_map(
        body,
        mesh=mesh,
        in_specs=(
            P("groups", ("ctx", "head"), None),
            P("groups", ("ctx", "head")),
            P(("ctx", "head"), None, None),
            P(("ctx", "head"), None, None),
            P(("ctx", "head"), None),
            P(("groups", "ctx"), None, None),
            P(("groups", "ctx")),
        ),
        out_specs=P("groups", ("ctx", "head")),
        check_vma=False,
    )
```

```python
import functools

import jax
import jax.numpy as jnp
from jax import lax
from jax.experimental import pallas as pl
from jax.experimental.pallas import tpu as pltpu
from jax.sharding import PartitionSpec as P

masked_score = -1e30
LANES = 128
GROUP_PAGES = 4
CACHE_PARTS = 2
MIB = 1024 * 1024

VMEM_SPEC = pl.BlockSpec(memory_space=pltpu.VMEM)
SMEM_SPEC = pl.BlockSpec(memory_space=pltpu.SMEM)


def in_vmem(x):
    return pltpu.with_memory_space_constraint(x, pltpu.VMEM)


def split_level(level):
    high = level.astype(jnp.bfloat16)
    rest = level - high.astype(jnp.float32)
    middle = rest.astype(jnp.bfloat16)
    low = (rest - middle.astype(jnp.float32)).astype(jnp.bfloat16)
    return high, middle, low


def store_level(message_ref, row, level):
    for i, part in enumerate(split_level(level)):
        message_ref[row, :, i * LANES : (i + 1) * LANES] = part


def load_level(message_ref, row):
    parts = [
        message_ref[row, :, i * LANES : (i + 1) * LANES].astype(jnp.float32) for i in range(3)
    ]
    return (parts[0] + parts[1]) + parts[2]


def load_kernel(first, cache_ref, after_ref, out_ref, sem):
    copy = pltpu.make_async_copy(cache_ref.at[pl.ds(first, out_ref.shape[0])], out_ref, sem)
    copy.start()
    copy.wait()


def load(cache, part, parts, after):
    pages = cache.shape[0] // parts
    return pl.pallas_call(
        functools.partial(load_kernel, part * pages),
        out_shape=pltpu.VMEM((pages, *cache.shape[1:]), cache.dtype),
        in_specs=[pl.BlockSpec(memory_space=pltpu.HBM), pl.BlockSpec(memory_space=pl.ANY)],
        out_specs=VMEM_SPEC,
        scratch_shapes=[pltpu.SemaphoreType.DMA],
        compiler_params=pltpu.CompilerParams(vmem_limit_bytes=MIB),
        cost_estimate=pl.CostEstimate(
            flops=0, bytes_accessed=2 * cache.size // parts, transcendentals=0
        ),
        name="load",
    )(pltpu.with_memory_space_constraint(cache, pltpu.HBM), after)


def attend_kernel(score_scale, steps, blocks, owner_ref, weight_ref, *refs):
    cache_refs, refs = refs[:CACHE_PARTS], refs[CACHE_PARTS:]
    query_refs, message_refs = refs[:blocks], refs[blocks : 2 * blocks]
    weight_out, query_scr, score_scr, max_scr, total_scr, sum_scr, weight_sem = refs[2 * blocks :]
    requests, heads, entry_size = query_scr.shape
    pages_part, page_len, _ = cache_refs[0].shape
    _, heads_here, latent_size = message_refs[0].shape
    rope_size = entry_size - latent_size
    ropes_row = latent_size // rope_size
    pair_len = 2 * page_len
    pair_count = GROUP_PAGES // 2
    groups_part = pages_part // GROUP_PAGES
    groups_step = groups_part // steps
    group_len = GROUP_PAGES * page_len

    weight_copy = pltpu.make_async_copy(weight_ref, weight_out, weight_sem)
    weight_copy.start()

    for b, ref in enumerate(query_refs):
        rows = slice(b * heads_here, (b + 1) * heads_here)
        for r in range(requests):
            start = r % ropes_row * rope_size
            query_scr[r, rows, :latent_size] = ref[r]
            query_scr[r, rows, latent_size:] = ref[requests + r // ropes_row][
                :, start : start + rope_size
            ]

    first_half = lax.broadcasted_iota(jnp.int32, (heads, pair_len), 1) < page_len

    for r in range(requests + 1):
        max_scr[r] = jnp.full((heads, pair_len), masked_score, jnp.float32)
        total_scr[r] = jnp.zeros((heads, pair_len), jnp.float32)
        sum_scr[r] = jnp.zeros((heads, latent_size), jnp.float32)

    def owners_of(g):
        raw = [owner_ref[g * GROUP_PAGES + k] for k in range(GROUP_PAGES)]
        return [jnp.where(o < 0, requests, o) for o in raw]

    def score_group(part, local):
        g = part * groups_part + local
        owners = owners_of(g)
        keys = cache_refs[part][pl.ds(local * GROUP_PAGES, GROUP_PAGES)].reshape(group_len, entry_size)
        queries = jnp.concatenate(
            [query_scr[jnp.minimum(o, requests - 1)] for o in owners], axis=0
        )
        scores = lax.dot_general(
            queries, keys, (((1,), (1,)), ((), ())), preferred_element_type=jnp.float32
        )
        for p in range(pair_count):
            left, right = 2 * p, 2 * p + 1
            columns = slice(p * pair_len, (p + 1) * pair_len)
            pair = score_scale * jnp.where(
                first_half,
                scores[left * heads : (left + 1) * heads, columns],
                scores[right * heads : (right + 1) * heads, columns],
            )
            score_scr[g * pair_count + p] = pair
            max_scr[owners[left]] = jnp.maximum(
                max_scr[owners[left]], jnp.where(first_half, pair, masked_score)
            )
            max_scr[owners[right]] = jnp.maximum(
                max_scr[owners[right]], jnp.where(first_half, masked_score, pair)
            )

    def score_step(part, c, carry):
        for i in range(groups_step):
            score_group(part, c * groups_step + i)
        return carry

    for part in range(CACHE_PARTS):
        lax.fori_loop(0, steps, functools.partial(score_step, part), 0)

    for r in range(requests + 1):
        top = jnp.max(max_scr[r], axis=1, keepdims=True)
        max_scr[r] = jnp.broadcast_to(top, (heads, pair_len))

    def sum_group(part, local):
        g = part * groups_part + local
        owners = owners_of(g)
        values = cache_refs[part][pl.ds(local * GROUP_PAGES, GROUP_PAGES)].reshape(group_len, entry_size)[
            :, :latent_size
        ]
        rows = []
        for p in range(pair_count):
            left, right = owners[2 * p], owners[2 * p + 1]
            offset = jnp.where(first_half, max_scr[left], max_scr[right])
            weight = jnp.exp(score_scr[g * pair_count + p] - offset)
            left_weight = jnp.where(first_half, weight, 0.0)
            right_weight = jnp.where(first_half, 0.0, weight)
            total_scr[left] += left_weight
            total_scr[right] += right_weight
            for part in (left_weight, right_weight):
                half = part.astype(jnp.bfloat16)
                pieces = [half if q == p else jnp.zeros_like(half) for q in range(pair_count)]
                rows.append(jnp.concatenate(pieces, axis=1))
        added = jnp.dot(
            jnp.concatenate(rows, axis=0), values, preferred_element_type=jnp.float32
        )
        for k in range(GROUP_PAGES):
            sum_scr[owners[k]] += added[k * heads : (k + 1) * heads]

    def sum_step(part, c, carry):
        for i in range(groups_step):
            sum_group(part, c * groups_step + i)
        return carry

    for part in range(CACHE_PARTS):
        lax.fori_loop(0, steps, functools.partial(sum_step, part), 0)

    lane = lax.broadcasted_iota(jnp.int32, (heads, LANES), 1)
    stats = jnp.full((heads, LANES), masked_score, jnp.float32)
    for r in range(requests):
        total = jnp.sum(total_scr[r], axis=1, keepdims=True)
        present = total > 0.0
        safe = jnp.where(present, total, 1.0)
        mean = (sum_scr[r] * (1.0 / safe)).astype(jnp.bfloat16)
        level = jnp.where(present, max_scr[r][:, :1] + jnp.log(safe), masked_score)
        stats = jnp.where(lane == r, level, stats)
        for b in range(blocks):
            message_refs[b][r] = mean[b * heads_here : (b + 1) * heads_here]
    for b in range(blocks):
        message_refs[b][requests] = jnp.zeros((heads_here, latent_size), jnp.bfloat16)
        store_level(message_refs[b], requests, stats[b * heads_here : (b + 1) * heads_here])
    weight_copy.wait()


def attend(query_blocks, cache_parts, page_owner, output_weight, score_scale, latent_size):
    pages_part, page_len, entry_size = cache_parts[0].shape
    pages = pages_part * CACHE_PARTS
    blocks = len(query_blocks)
    heads_here = query_blocks[0].shape[1]
    requests = query_blocks[0].shape[0] * latent_size // entry_size
    heads = heads_here * blocks
    pair_len = 2 * page_len
    groups = pages_part // GROUP_PAGES
    steps = groups // max(d for d in range(1, 15) if groups % d == 0)
    out = pl.pallas_call(
        functools.partial(attend_kernel, score_scale, steps, blocks),
        out_shape=[
            pltpu.VMEM((requests + 1, heads_here, latent_size), jnp.bfloat16)
            for _ in range(blocks)
        ]
        + [pltpu.VMEM(output_weight.shape, output_weight.dtype)],
        in_specs=[SMEM_SPEC, pl.BlockSpec(memory_space=pl.ANY)]
        + [VMEM_SPEC] * (CACHE_PARTS + blocks),
        out_specs=[VMEM_SPEC] * (blocks + 1),
        scratch_shapes=[
            pltpu.VMEM((requests, heads, entry_size), jnp.bfloat16),
            pltpu.VMEM((pages // 2, heads, pair_len), jnp.float32),
            pltpu.VMEM((requests + 1, heads, pair_len), jnp.float32),
            pltpu.VMEM((requests + 1, heads, pair_len), jnp.float32),
            pltpu.VMEM((requests + 1, heads, latent_size), jnp.float32),
            pltpu.SemaphoreType.DMA,
        ],
        compiler_params=pltpu.CompilerParams(vmem_limit_bytes=16 * MIB),
        cost_estimate=pl.CostEstimate(
            flops=2 * pages * page_len * heads * (entry_size + latent_size) * 4,
            bytes_accessed=pages * page_len * entry_size * 2,
            transcendentals=pages * page_len * heads,
        ),
        name="attend",
    )(page_owner, output_weight, *map(in_vmem, [*cache_parts, *query_blocks]))
    return list(out[:-1]), out[-1]


def shares(levels):
    top = functools.reduce(jnp.maximum, levels)
    parts = [jnp.exp(level - top) for level in levels]
    total = functools.reduce(jnp.add, parts)
    return [part / total for part in parts], top + jnp.log(total)


def merge_kernel(own_ref, got_ref, out_ref):
    requests = own_ref.shape[0] - 1
    both = (own_ref, got_ref)
    weights, level = shares([load_level(ref, requests) for ref in both])
    for r in range(requests):
        out_ref[r] = sum(
            w[:, r : r + 1] * ref[r].astype(jnp.float32) for w, ref in zip(weights, both)
        ).astype(jnp.bfloat16)
    out_ref[requests] = jnp.zeros(out_ref.shape[1:], jnp.bfloat16)
    store_level(out_ref, requests, level)


def merge(own, got):
    return pl.pallas_call(
        merge_kernel,
        out_shape=pltpu.VMEM(own.shape, own.dtype),
        in_specs=[VMEM_SPEC] * 2,
        out_specs=VMEM_SPEC,
        compiler_params=pltpu.CompilerParams(vmem_limit_bytes=2 * MIB),
        cost_estimate=pl.CostEstimate(flops=4 * own.size, bytes_accessed=0, transcendentals=0),
        name="merge",
    )(in_vmem(own), in_vmem(got))


def finish_kernel(
    block_columns, radices, here_ref, value_ref, weight_ref, *refs
):
    messages, (out_ref, attended_scr, head_scr) = refs[:-3], refs[-3:]
    requests, heads_here = messages[0].shape[0] - 1, messages[0].shape[1]
    value_size = value_ref.shape[2]
    owners, _, width = out_ref.shape
    weights, _ = shares([load_level(ref, requests) for ref in messages])
    for r in range(requests):
        attended_scr[r * heads_here : (r + 1) * heads_here] = sum(
            w[:, r : r + 1] * ref[r].astype(jnp.float32) for w, ref in zip(weights, messages)
        )
    attended = attended_scr[...].astype(jnp.bfloat16)
    row = lax.broadcasted_iota(jnp.int32, (requests, requests * heads_here), 0)
    column = lax.broadcasted_iota(jnp.int32, (requests, requests * heads_here), 1)
    for h in range(heads_here):
        pick = jnp.where(column == row * heads_here + h, 1.0, 0.0).astype(jnp.bfloat16)
        rows = jnp.dot(pick, attended, preferred_element_type=jnp.float32).astype(jnp.bfloat16)
        head_scr[:, h * value_size : (h + 1) * value_size] = jnp.dot(
            rows, value_ref[h], preferred_element_type=jnp.float32
        ).astype(jnp.bfloat16)
    head_out = head_scr[...]
    per_block = block_columns // width
    for j in range(owners // per_block):
        product = jnp.dot(
            head_out,
            weight_ref[:, j * block_columns : (j + 1) * block_columns],
            preferred_element_type=jnp.float32,
        ).astype(jnp.bfloat16)
        for i in range(per_block):
            distance = here_ref[0] ^ (j * per_block + i)
            place = 0
            for radix in radices:
                place = place * radix + (distance & (radix - 1))
                distance = distance >> (radix.bit_length() - 1)
            out_ref[place] = product[:, i * width : (i + 1) * width]


def finish(here, messages, value_absorb, weight, radices):
    requests, heads_here = messages[0].shape[0] - 1, messages[0].shape[1]
    latent_size, value_size = value_absorb.shape[1:]
    depth, columns = weight.shape
    owners = functools.reduce(lambda a, b: a * b, radices)
    width = columns // owners
    block_columns = width
    while block_columns % LANES:
        block_columns *= 2
    return pl.pallas_call(
        functools.partial(finish_kernel, block_columns, radices),
        out_shape=pltpu.VMEM((owners, requests, width), jnp.bfloat16),
        in_specs=[SMEM_SPEC] + [VMEM_SPEC] * (2 + len(messages)),
        out_specs=VMEM_SPEC,
        scratch_shapes=[
            pltpu.VMEM((requests * heads_here, latent_size), jnp.float32),
            pltpu.VMEM((requests, heads_here * value_size), jnp.bfloat16),
        ],
        compiler_params=pltpu.CompilerParams(vmem_limit_bytes=8 * MIB),
        cost_estimate=pl.CostEstimate(
            flops=2 * 256 * depth * columns, bytes_accessed=0, transcendentals=0
        ),
        name="finish",
    )(here, *[in_vmem(x) for x in (value_absorb, weight, *messages)])


def body(
    query_nope, query_rope, key_absorb, value_absorb, output_weight, latent_cache, page_owner
):
    requests, heads_here, nope_size = query_nope.shape
    latent_size = key_absorb.shape[2]
    rope_size = query_rope.shape[1] // heads_here
    score_scale = (nope_size + rope_size) ** (-0.5)
    count = lax.axis_size("ctx")
    axes = ("ctx", "head")
    here = lax.axis_index(axes).astype(jnp.int32).reshape(1)

    def exchange(x, distance):
        return lax.ppermute(x, "ctx", [(i, i ^ distance) for i in range(count)])

    query_latent = jnp.einsum(
        "rhn,hnl->rhl", query_nope, key_absorb, preferred_element_type=jnp.float32
    ).astype(jnp.bfloat16)
    ropes_row = latent_size // rope_size
    rope = query_rope.reshape(-1, ropes_row, heads_here, rope_size).transpose(0, 2, 1, 3)
    own = jnp.concatenate([query_latent, rope.reshape(-1, heads_here, latent_size)], axis=0)
    own, here = lax.optimization_barrier((own, here))

    bits = [1 << b for b in range(count.bit_length() - 1)]
    block_at = {0: own}
    for bit in reversed(bits):
        for distance in list(block_at):
            block_at[distance ^ bit] = exchange(block_at[distance], bit)

    cache_parts = [
        load(latent_cache, i, CACHE_PARTS, block) for i, block in enumerate([own, block_at[bits[-1]]])
    ]
    message_to, weight = attend(
        [block_at[d] for d in range(count)],
        cache_parts, page_owner, output_weight, score_scale, latent_size,
    )

    messages = [message_to[0]]
    for bit in bits:
        for distance in range(count - bit, 0, -2 * bit):
            got = exchange(message_to[distance], bit)
            if distance == bit:
                messages.append(got)
            else:
                message_to[distance ^ bit] = merge(message_to[distance ^ bit], got)

    owners = lax.axis_size(axes)
    radices = []
    while functools.reduce(lambda a, b: a * b, radices, 1) < owners:
        left = owners // functools.reduce(lambda a, b: a * b, radices, 1)
        radices.append(4 if left % 4 == 0 else 2)
    pieces = finish(here, messages, value_absorb, weight, radices)
    unit = 1
    for radix in radices:
        share = pieces.shape[0] // radix
        got = [
            lax.ppermute(
                pieces[k * share : (k + 1) * share],
                axes,
                [(i, i ^ (k * unit)) for i in range(owners)],
            )
            for k in range(1, radix)
        ]
        pieces = sum(x.astype(jnp.float32) for x in [pieces[:share], *got]).astype(jnp.bfloat16)
        unit *= radix
    return pieces[0]


def solution(mesh):
    return jax.shard_map(
        body,
        mesh=mesh,
        in_specs=(
            P("groups", ("ctx", "head"), None),
            P("groups", ("ctx", "head")),
            P(("ctx", "head"), None, None),
            P(("ctx", "head"), None, None),
            P(("ctx", "head"), None),
            P(("groups", "ctx"), None, None),
            P(("groups", "ctx")),
        ),
        out_specs=P("groups", ("ctx", "head")),
        check_vma=False,
    )
```

```python
import functools

import jax
import jax.numpy as jnp
from jax import lax
from jax.experimental import pallas as pl
from jax.experimental.pallas import tpu as pltpu
from jax.sharding import PartitionSpec as P

masked_score = -1e30
LANES = 128
GROUP_PAGES = 4
CACHE_PARTS = 2
MIB = 1024 * 1024

VMEM_SPEC = pl.BlockSpec(memory_space=pltpu.VMEM)
SMEM_SPEC = pl.BlockSpec(memory_space=pltpu.SMEM)


def in_vmem(x):
    return pltpu.with_memory_space_constraint(x, pltpu.VMEM)


def split_level(level):
    high = level.astype(jnp.bfloat16)
    rest = level - high.astype(jnp.float32)
    middle = rest.astype(jnp.bfloat16)
    low = (rest - middle.astype(jnp.float32)).astype(jnp.bfloat16)
    return high, middle, low


def store_level(message_ref, row, level):
    for i, part in enumerate(split_level(level)):
        message_ref[row, :, i * LANES : (i + 1) * LANES] = part


def load_level(message_ref, row):
    parts = [
        message_ref[row, :, i * LANES : (i + 1) * LANES].astype(jnp.float32) for i in range(3)
    ]
    return (parts[0] + parts[1]) + parts[2]


def load_kernel(first, cache_ref, after_ref, out_ref, sem):
    copy = pltpu.make_async_copy(cache_ref.at[pl.ds(first, out_ref.shape[0])], out_ref, sem)
    copy.start()
    copy.wait()


def load(cache, part, parts, after):
    pages = cache.shape[0] // parts
    return pl.pallas_call(
        functools.partial(load_kernel, part * pages),
        out_shape=pltpu.VMEM((pages, *cache.shape[1:]), cache.dtype),
        in_specs=[pl.BlockSpec(memory_space=pltpu.HBM), pl.BlockSpec(memory_space=pl.ANY)],
        out_specs=VMEM_SPEC,
        scratch_shapes=[pltpu.SemaphoreType.DMA],
        compiler_params=pltpu.CompilerParams(vmem_limit_bytes=MIB),
        cost_estimate=pl.CostEstimate(
            flops=0, bytes_accessed=2 * cache.size // parts, transcendentals=0
        ),
        name="load",
    )(pltpu.with_memory_space_constraint(cache, pltpu.HBM), after)


def pass_kernel(others, here_ref, *refs):
    refs[others][0] = here_ref[0]


def gate(here, blocks, after):
    any_spec = pl.BlockSpec(memory_space=pl.ANY)
    out = pl.pallas_call(
        functools.partial(pass_kernel, len(blocks) + 1),
        out_shape=[
            jax.ShapeDtypeStruct(here.shape, here.dtype),
            *[jax.ShapeDtypeStruct(x.shape, x.dtype) for x in blocks],
        ],
        in_specs=[SMEM_SPEC] + [any_spec] * (len(blocks) + 1),
        out_specs=[SMEM_SPEC] + [any_spec] * len(blocks),
        input_output_aliases={i + 1: i + 1 for i in range(len(blocks))},
        compiler_params=pltpu.CompilerParams(vmem_limit_bytes=MIB),
        cost_estimate=pl.CostEstimate(flops=0, bytes_accessed=0, transcendentals=0),
        name="gate",
    )(here, *blocks, after)
    return out[0], list(out[1:])


def attend_kernel(score_scale, steps, blocks, owner_ref, weight_ref, *refs):
    cache_refs, refs = refs[:CACHE_PARTS], refs[CACHE_PARTS:]
    query_refs, message_refs = refs[:blocks], refs[blocks : 2 * blocks]
    weight_out, query_scr, score_scr, max_scr, total_scr, sum_scr, weight_sem = refs[2 * blocks :]
    requests, heads, entry_size = query_scr.shape
    pages_part, page_len, _ = cache_refs[0].shape
    _, heads_here, latent_size = message_refs[0].shape
    rope_size = entry_size - latent_size
    ropes_row = latent_size // rope_size
    pair_len = 2 * page_len
    pair_count = GROUP_PAGES // 2
    groups_part = pages_part // GROUP_PAGES
    groups_step = groups_part // steps
    group_len = GROUP_PAGES * page_len

    weight_copy = pltpu.make_async_copy(weight_ref, weight_out, weight_sem)
    weight_copy.start()

    for b, ref in enumerate(query_refs):
        rows = slice(b * heads_here, (b + 1) * heads_here)
        for r in range(requests):
            start = r % ropes_row * rope_size
            query_scr[r, rows, :latent_size] = ref[r]
            query_scr[r, rows, latent_size:] = ref[requests + r // ropes_row][
                :, start : start + rope_size
            ]

    first_half = lax.broadcasted_iota(jnp.int32, (heads, pair_len), 1) < page_len

    for r in range(requests + 1):
        max_scr[r] = jnp.full((heads, pair_len), masked_score, jnp.float32)
        total_scr[r] = jnp.zeros((heads, pair_len), jnp.float32)
        sum_scr[r] = jnp.zeros((heads, latent_size), jnp.float32)

    def owners_of(g):
        raw = [owner_ref[g * GROUP_PAGES + k] for k in range(GROUP_PAGES)]
        return [jnp.where(o < 0, requests, o) for o in raw]

    def score_group(part, local):
        g = part * groups_part + local
        owners = owners_of(g)
        keys = cache_refs[part][pl.ds(local * GROUP_PAGES, GROUP_PAGES)].reshape(group_len, entry_size)
        queries = jnp.concatenate(
            [query_scr[jnp.minimum(o, requests - 1)] for o in owners], axis=0
        )
        scores = lax.dot_general(
            queries, keys, (((1,), (1,)), ((), ())), preferred_element_type=jnp.float32
        )
        for p in range(pair_count):
            left, right = 2 * p, 2 * p + 1
            columns = slice(p * pair_len, (p + 1) * pair_len)
            pair = score_scale * jnp.where(
                first_half,
                scores[left * heads : (left + 1) * heads, columns],
                scores[right * heads : (right + 1) * heads, columns],
            )
            score_scr[g * pair_count + p] = pair
            max_scr[owners[left]] = jnp.maximum(
                max_scr[owners[left]], jnp.where(first_half, pair, masked_score)
            )
            max_scr[owners[right]] = jnp.maximum(
                max_scr[owners[right]], jnp.where(first_half, masked_score, pair)
            )

    def score_step(part, c, carry):
        for i in range(groups_step):
            score_group(part, c * groups_step + i)
        return carry

    for part in range(CACHE_PARTS):
        lax.fori_loop(0, steps, functools.partial(score_step, part), 0)

    for r in range(requests + 1):
        top = jnp.max(max_scr[r], axis=1, keepdims=True)
        max_scr[r] = jnp.broadcast_to(top, (heads, pair_len))

    def sum_group(part, local):
        g = part * groups_part + local
        owners = owners_of(g)
        values = cache_refs[part][pl.ds(local * GROUP_PAGES, GROUP_PAGES)].reshape(group_len, entry_size)[
            :, :latent_size
        ]
        rows = []
        for p in range(pair_count):
            left, right = owners[2 * p], owners[2 * p + 1]
            offset = jnp.where(first_half, max_scr[left], max_scr[right])
            weight = jnp.exp(score_scr[g * pair_count + p] - offset)
            left_weight = jnp.where(first_half, weight, 0.0)
            right_weight = jnp.where(first_half, 0.0, weight)
            total_scr[left] += left_weight
            total_scr[right] += right_weight
            for part in (left_weight, right_weight):
                half = part.astype(jnp.bfloat16)
                pieces = [half if q == p else jnp.zeros_like(half) for q in range(pair_count)]
                rows.append(jnp.concatenate(pieces, axis=1))
        added = jnp.dot(
            jnp.concatenate(rows, axis=0), values, preferred_element_type=jnp.float32
        )
        for k in range(GROUP_PAGES):
            sum_scr[owners[k]] += added[k * heads : (k + 1) * heads]

    def sum_step(part, c, carry):
        for i in range(groups_step):
            sum_group(part, c * groups_step + i)
        return carry

    for part in range(CACHE_PARTS):
        lax.fori_loop(0, steps, functools.partial(sum_step, part), 0)

    lane = lax.broadcasted_iota(jnp.int32, (heads, LANES), 1)
    stats = jnp.full((heads, LANES), masked_score, jnp.float32)
    for r in range(requests):
        total = jnp.sum(total_scr[r], axis=1, keepdims=True)
        present = total > 0.0
        safe = jnp.where(present, total, 1.0)
        mean = (sum_scr[r] * (1.0 / safe)).astype(jnp.bfloat16)
        level = jnp.where(present, max_scr[r][:, :1] + jnp.log(safe), masked_score)
        stats = jnp.where(lane == r, level, stats)
        for b in range(blocks):
            message_refs[b][r] = mean[b * heads_here : (b + 1) * heads_here]
    for b in range(blocks):
        message_refs[b][requests] = jnp.zeros((heads_here, latent_size), jnp.bfloat16)
        store_level(message_refs[b], requests, stats[b * heads_here : (b + 1) * heads_here])
    weight_copy.wait()


def attend(query_blocks, cache_parts, page_owner, output_weight, score_scale, latent_size):
    pages_part, page_len, entry_size = cache_parts[0].shape
    pages = pages_part * CACHE_PARTS
    blocks = len(query_blocks)
    heads_here = query_blocks[0].shape[1]
    requests = query_blocks[0].shape[0] * latent_size // entry_size
    heads = heads_here * blocks
    pair_len = 2 * page_len
    groups = pages_part // GROUP_PAGES
    steps = groups // max(d for d in range(1, 15) if groups % d == 0)
    out = pl.pallas_call(
        functools.partial(attend_kernel, score_scale, steps, blocks),
        out_shape=[
            pltpu.VMEM((requests + 1, heads_here, latent_size), jnp.bfloat16)
            for _ in range(blocks)
        ]
        + [pltpu.VMEM(output_weight.shape, output_weight.dtype)],
        in_specs=[SMEM_SPEC, pl.BlockSpec(memory_space=pl.ANY)]
        + [VMEM_SPEC] * (CACHE_PARTS + blocks),
        out_specs=[VMEM_SPEC] * (blocks + 1),
        scratch_shapes=[
            pltpu.VMEM((requests, heads, entry_size), jnp.bfloat16),
            pltpu.VMEM((pages // 2, heads, pair_len), jnp.float32),
            pltpu.VMEM((requests + 1, heads, pair_len), jnp.float32),
            pltpu.VMEM((requests + 1, heads, pair_len), jnp.float32),
            pltpu.VMEM((requests + 1, heads, latent_size), jnp.float32),
            pltpu.SemaphoreType.DMA,
        ],
        compiler_params=pltpu.CompilerParams(vmem_limit_bytes=16 * MIB),
        cost_estimate=pl.CostEstimate(
            flops=2 * pages * page_len * heads * (entry_size + latent_size) * 4,
            bytes_accessed=pages * page_len * entry_size * 2,
            transcendentals=pages * page_len * heads,
        ),
        name="attend",
    )(page_owner, output_weight, *map(in_vmem, [*cache_parts, *query_blocks]))
    return list(out[:-1]), out[-1]


def shares(levels):
    top = functools.reduce(jnp.maximum, levels)
    parts = [jnp.exp(level - top) for level in levels]
    total = functools.reduce(jnp.add, parts)
    return [part / total for part in parts], top + jnp.log(total)


def merge_kernel(own_ref, got_ref, out_ref):
    requests = own_ref.shape[0] - 1
    both = (own_ref, got_ref)
    weights, level = shares([load_level(ref, requests) for ref in both])
    for r in range(requests):
        out_ref[r] = sum(
            w[:, r : r + 1] * ref[r].astype(jnp.float32) for w, ref in zip(weights, both)
        ).astype(jnp.bfloat16)
    out_ref[requests] = jnp.zeros(out_ref.shape[1:], jnp.bfloat16)
    store_level(out_ref, requests, level)


def merge(own, got):
    return pl.pallas_call(
        merge_kernel,
        out_shape=pltpu.VMEM(own.shape, own.dtype),
        in_specs=[VMEM_SPEC] * 2,
        out_specs=VMEM_SPEC,
        compiler_params=pltpu.CompilerParams(vmem_limit_bytes=2 * MIB),
        cost_estimate=pl.CostEstimate(flops=4 * own.size, bytes_accessed=0, transcendentals=0),
        name="merge",
    )(in_vmem(own), in_vmem(got))


def finish_kernel(
    block_columns, radices, here_ref, value_ref, weight_ref, *refs
):
    messages, (out_ref, attended_scr, head_scr) = refs[:-3], refs[-3:]
    requests, heads_here = messages[0].shape[0] - 1, messages[0].shape[1]
    value_size = value_ref.shape[2]
    owners, _, width = out_ref.shape
    weights, _ = shares([load_level(ref, requests) for ref in messages])
    for r in range(requests):
        attended_scr[r * heads_here : (r + 1) * heads_here] = sum(
            w[:, r : r + 1] * ref[r].astype(jnp.float32) for w, ref in zip(weights, messages)
        )
    attended = attended_scr[...].astype(jnp.bfloat16)
    row = lax.broadcasted_iota(jnp.int32, (requests, requests * heads_here), 0)
    column = lax.broadcasted_iota(jnp.int32, (requests, requests * heads_here), 1)
    for h in range(heads_here):
        pick = jnp.where(column == row * heads_here + h, 1.0, 0.0).astype(jnp.bfloat16)
        rows = jnp.dot(pick, attended, preferred_element_type=jnp.float32).astype(jnp.bfloat16)
        head_scr[:, h * value_size : (h + 1) * value_size] = jnp.dot(
            rows, value_ref[h], preferred_element_type=jnp.float32
        ).astype(jnp.bfloat16)
    head_out = head_scr[...]
    per_block = block_columns // width
    for j in range(owners // per_block):
        product = jnp.dot(
            head_out,
            weight_ref[:, j * block_columns : (j + 1) * block_columns],
            preferred_element_type=jnp.float32,
        ).astype(jnp.bfloat16)
        for i in range(per_block):
            distance = here_ref[0] ^ (j * per_block + i)
            place = 0
            for radix in radices:
                place = place * radix + (distance & (radix - 1))
                distance = distance >> (radix.bit_length() - 1)
            out_ref[place] = product[:, i * width : (i + 1) * width]


def finish(here, messages, value_absorb, weight, radices):
    requests, heads_here = messages[0].shape[0] - 1, messages[0].shape[1]
    latent_size, value_size = value_absorb.shape[1:]
    depth, columns = weight.shape
    owners = functools.reduce(lambda a, b: a * b, radices)
    width = columns // owners
    block_columns = width
    while block_columns % LANES:
        block_columns *= 2
    return pl.pallas_call(
        functools.partial(finish_kernel, block_columns, radices),
        out_shape=pltpu.VMEM((owners, requests, width), jnp.bfloat16),
        in_specs=[SMEM_SPEC] + [VMEM_SPEC] * (2 + len(messages)),
        out_specs=VMEM_SPEC,
        scratch_shapes=[
            pltpu.VMEM((requests * heads_here, latent_size), jnp.float32),
            pltpu.VMEM((requests, heads_here * value_size), jnp.bfloat16),
        ],
        compiler_params=pltpu.CompilerParams(vmem_limit_bytes=8 * MIB),
        cost_estimate=pl.CostEstimate(
            flops=2 * 256 * depth * columns, bytes_accessed=0, transcendentals=0
        ),
        name="finish",
    )(here, *[in_vmem(x) for x in (value_absorb, weight, *messages)])


def body(
    query_nope, query_rope, key_absorb, value_absorb, output_weight, latent_cache, page_owner
):
    requests, heads_here, nope_size = query_nope.shape
    latent_size = key_absorb.shape[2]
    rope_size = query_rope.shape[1] // heads_here
    score_scale = (nope_size + rope_size) ** (-0.5)
    count = lax.axis_size("ctx")
    axes = ("ctx", "head")
    here = lax.axis_index(axes).astype(jnp.int32).reshape(1)

    def exchange(x, distance):
        return lax.ppermute(x, "ctx", [(i, i ^ distance) for i in range(count)])

    query_latent = jnp.einsum(
        "rhn,hnl->rhl", query_nope, key_absorb, preferred_element_type=jnp.float32
    ).astype(jnp.bfloat16)
    ropes_row = latent_size // rope_size
    rope = query_rope.reshape(-1, ropes_row, heads_here, rope_size).transpose(0, 2, 1, 3)
    own = jnp.concatenate([query_latent, rope.reshape(-1, heads_here, latent_size)], axis=0)

    bits = [1 << b for b in reversed(range(count.bit_length() - 1))]
    block_at = {bit: exchange(own, bit) for bit in bits}
    cache_parts = [load(latent_cache, 0, CACHE_PARTS, own)]
    here, passed = gate(here, list(block_at.values()), cache_parts[0])
    block_at = {0: own, **dict(zip(bits, passed))}
    for distance in sorted(range(count), key=lambda d: (d.bit_count(), -d)):
        if distance.bit_count() > 1:
            bit = distance & -distance
            block_at[distance] = exchange(block_at[distance ^ bit], bit)
    for part in range(1, CACHE_PARTS):
        cache_parts.append(load(latent_cache, part, CACHE_PARTS, block_at[bits[0]]))

    message_to, weight = attend(
        [block_at[d] for d in range(count)],
        cache_parts, page_owner, output_weight, score_scale, latent_size,
    )

    even = [*range(4, count, 2), *range(2, min(4, count), 2)]
    across = {distance: exchange(message_to[distance ^ 1], 1) for distance in [*even, 0]}
    arrived = [
        exchange(merge(message_to[distance], across[distance]), distance) for distance in even
    ]
    messages = [message_to[0], across[0], *arrived]

    owners = lax.axis_size(axes)
    radices = [owners // count, count]
    pieces = finish(here, messages, value_absorb, weight, radices)
    unit = 1
    for radix in radices:
        share = pieces.shape[0] // radix
        got = [
            lax.ppermute(
                pieces[k * share : (k + 1) * share],
                axes,
                [(i, i ^ (k * unit)) for i in range(owners)],
            )
            for k in range(1, radix)
        ]
        pieces = sum(x.astype(jnp.float32) for x in [pieces[:share], *got]).astype(jnp.bfloat16)
        unit *= radix
    return pieces[0]


def solution(mesh):
    return jax.shard_map(
        body,
        mesh=mesh,
        in_specs=(
            P("groups", ("ctx", "head"), None),
            P("groups", ("ctx", "head")),
            P(("ctx", "head"), None, None),
            P(("ctx", "head"), None, None),
            P(("ctx", "head"), None),
            P(("groups", "ctx"), None, None),
            P(("groups", "ctx")),
        ),
        out_specs=P("groups", ("ctx", "head")),
        check_vma=False,
    )
```

```python
import functools

import jax
import jax.numpy as jnp
from jax import lax
from jax.experimental import pallas as pl
from jax.experimental.pallas import tpu as pltpu
from jax.sharding import PartitionSpec as P

masked_score = -1e30
LANES = 128
GROUP_PAGES = 4
CACHE_PARTS = 2
MIB = 1024 * 1024

VMEM_SPEC = pl.BlockSpec(memory_space=pltpu.VMEM)
SMEM_SPEC = pl.BlockSpec(memory_space=pltpu.SMEM)


def in_vmem(x):
    return pltpu.with_memory_space_constraint(x, pltpu.VMEM)


def split_level(level):
    high = level.astype(jnp.bfloat16)
    rest = level - high.astype(jnp.float32)
    middle = rest.astype(jnp.bfloat16)
    low = (rest - middle.astype(jnp.float32)).astype(jnp.bfloat16)
    return high, middle, low


def store_level(message_ref, row, level):
    for i, part in enumerate(split_level(level)):
        message_ref[row, :, i * LANES : (i + 1) * LANES] = part


def load_level(message_ref, row):
    parts = [
        message_ref[row, :, i * LANES : (i + 1) * LANES].astype(jnp.float32) for i in range(3)
    ]
    return (parts[0] + parts[1]) + parts[2]


def load_kernel(first, here_ref, cache_ref, after_ref, out_ref, sem):
    copy = pltpu.make_async_copy(cache_ref.at[pl.ds(first, out_ref.shape[0])], out_ref, sem)
    copy.start()
    copy.wait()


def load(here, cache, part, parts, after):
    pages = cache.shape[0] // parts
    return pl.pallas_call(
        functools.partial(load_kernel, part * pages),
        out_shape=pltpu.VMEM((pages, *cache.shape[1:]), cache.dtype),
        in_specs=[
            SMEM_SPEC,
            pl.BlockSpec(memory_space=pltpu.HBM),
            pl.BlockSpec(memory_space=pl.ANY),
        ],
        out_specs=VMEM_SPEC,
        scratch_shapes=[pltpu.SemaphoreType.DMA],
        compiler_params=pltpu.CompilerParams(vmem_limit_bytes=MIB),
        cost_estimate=pl.CostEstimate(
            flops=0, bytes_accessed=2 * cache.size // parts, transcendentals=0
        ),
        name="load",
    )(here, pltpu.with_memory_space_constraint(cache, pltpu.HBM), after)


def pass_kernel(others, here_ref, *refs):
    refs[others][0] = here_ref[0]


def gate(here, blocks, after):
    any_spec = pl.BlockSpec(memory_space=pl.ANY)
    out = pl.pallas_call(
        functools.partial(pass_kernel, len(blocks) + 1),
        out_shape=[
            jax.ShapeDtypeStruct(here.shape, here.dtype),
            *[jax.ShapeDtypeStruct(x.shape, x.dtype) for x in blocks],
        ],
        in_specs=[SMEM_SPEC] + [any_spec] * (len(blocks) + 1),
        out_specs=[SMEM_SPEC] + [any_spec] * len(blocks),
        input_output_aliases={i + 1: i + 1 for i in range(len(blocks))},
        compiler_params=pltpu.CompilerParams(vmem_limit_bytes=MIB),
        cost_estimate=pl.CostEstimate(flops=0, bytes_accessed=0, transcendentals=0),
        name="gate",
    )(here, *blocks, after)
    return out[0], list(out[1:])


def attend_kernel(score_scale, steps, blocks, owner_ref, weight_ref, *refs):
    cache_refs, refs = refs[:CACHE_PARTS], refs[CACHE_PARTS:]
    query_refs, message_refs = refs[:blocks], refs[blocks : 2 * blocks]
    weight_out, query_scr, score_scr, max_scr, total_scr, sum_scr, weight_sem = refs[2 * blocks :]
    requests, heads, entry_size = query_scr.shape
    pages_part, page_len, _ = cache_refs[0].shape
    _, heads_here, latent_size = message_refs[0].shape
    rope_size = entry_size - latent_size
    ropes_row = latent_size // rope_size
    pair_len = 2 * page_len
    pair_count = GROUP_PAGES // 2
    groups_part = pages_part // GROUP_PAGES
    groups_step = groups_part // steps
    group_len = GROUP_PAGES * page_len

    weight_copy = pltpu.make_async_copy(weight_ref, weight_out, weight_sem)
    weight_copy.start()

    for b, ref in enumerate(query_refs):
        rows = slice(b * heads_here, (b + 1) * heads_here)
        for r in range(requests):
            start = r % ropes_row * rope_size
            query_scr[r, rows, :latent_size] = ref[r]
            query_scr[r, rows, latent_size:] = ref[requests + r // ropes_row][
                :, start : start + rope_size
            ]

    first_half = lax.broadcasted_iota(jnp.int32, (heads, pair_len), 1) < page_len

    for r in range(requests + 1):
        max_scr[r] = jnp.full((heads, pair_len), masked_score, jnp.float32)
        total_scr[r] = jnp.zeros((heads, pair_len), jnp.float32)
        sum_scr[r] = jnp.zeros((heads, latent_size), jnp.float32)

    def owners_of(g):
        raw = [owner_ref[g * GROUP_PAGES + k] for k in range(GROUP_PAGES)]
        return [jnp.where(o < 0, requests, o) for o in raw]

    def score_group(part, local):
        g = part * groups_part + local
        owners = owners_of(g)
        keys = cache_refs[part][pl.ds(local * GROUP_PAGES, GROUP_PAGES)].reshape(group_len, entry_size)
        queries = jnp.concatenate(
            [query_scr[jnp.minimum(o, requests - 1)] for o in owners], axis=0
        )
        scores = lax.dot_general(
            queries, keys, (((1,), (1,)), ((), ())), preferred_element_type=jnp.float32
        )
        for p in range(pair_count):
            left, right = 2 * p, 2 * p + 1
            columns = slice(p * pair_len, (p + 1) * pair_len)
            pair = score_scale * jnp.where(
                first_half,
                scores[left * heads : (left + 1) * heads, columns],
                scores[right * heads : (right + 1) * heads, columns],
            )
            score_scr[g * pair_count + p] = pair
            max_scr[owners[left]] = jnp.maximum(
                max_scr[owners[left]], jnp.where(first_half, pair, masked_score)
            )
            max_scr[owners[right]] = jnp.maximum(
                max_scr[owners[right]], jnp.where(first_half, masked_score, pair)
            )

    def score_step(part, c, carry):
        for i in range(groups_step):
            score_group(part, c * groups_step + i)
        return carry

    for part in range(CACHE_PARTS):
        lax.fori_loop(0, steps, functools.partial(score_step, part), 0)

    for r in range(requests + 1):
        top = jnp.max(max_scr[r], axis=1, keepdims=True)
        max_scr[r] = jnp.broadcast_to(top, (heads, pair_len))

    def sum_group(part, local):
        g = part * groups_part + local
        owners = owners_of(g)
        values = cache_refs[part][pl.ds(local * GROUP_PAGES, GROUP_PAGES)].reshape(group_len, entry_size)[
            :, :latent_size
        ]
        rows = []
        for p in range(pair_count):
            left, right = owners[2 * p], owners[2 * p + 1]
            offset = jnp.where(first_half, max_scr[left], max_scr[right])
            weight = jnp.exp(score_scr[g * pair_count + p] - offset)
            left_weight = jnp.where(first_half, weight, 0.0)
            right_weight = jnp.where(first_half, 0.0, weight)
            total_scr[left] += left_weight
            total_scr[right] += right_weight
            for part in (left_weight, right_weight):
                half = part.astype(jnp.bfloat16)
                pieces = [half if q == p else jnp.zeros_like(half) for q in range(pair_count)]
                rows.append(jnp.concatenate(pieces, axis=1))
        added = jnp.dot(
            jnp.concatenate(rows, axis=0), values, preferred_element_type=jnp.float32
        )
        for k in range(GROUP_PAGES):
            sum_scr[owners[k]] += added[k * heads : (k + 1) * heads]

    def sum_step(part, c, carry):
        for i in range(groups_step):
            sum_group(part, c * groups_step + i)
        return carry

    for part in range(CACHE_PARTS):
        lax.fori_loop(0, steps, functools.partial(sum_step, part), 0)

    lane = lax.broadcasted_iota(jnp.int32, (heads, LANES), 1)
    stats = jnp.full((heads, LANES), masked_score, jnp.float32)
    for r in range(requests):
        total = jnp.sum(total_scr[r], axis=1, keepdims=True)
        present = total > 0.0
        safe = jnp.where(present, total, 1.0)
        mean = (sum_scr[r] * (1.0 / safe)).astype(jnp.bfloat16)
        level = jnp.where(present, max_scr[r][:, :1] + jnp.log(safe), masked_score)
        stats = jnp.where(lane == r, level, stats)
        for b in range(blocks):
            message_refs[b][r] = mean[b * heads_here : (b + 1) * heads_here]
    for b in range(blocks):
        message_refs[b][requests] = jnp.zeros((heads_here, latent_size), jnp.bfloat16)
        store_level(message_refs[b], requests, stats[b * heads_here : (b + 1) * heads_here])
    weight_copy.wait()


def attend(query_blocks, cache_parts, page_owner, output_weight, score_scale, latent_size):
    pages_part, page_len, entry_size = cache_parts[0].shape
    pages = pages_part * CACHE_PARTS
    blocks = len(query_blocks)
    heads_here = query_blocks[0].shape[1]
    requests = query_blocks[0].shape[0] * latent_size // entry_size
    heads = heads_here * blocks
    pair_len = 2 * page_len
    groups = pages_part // GROUP_PAGES
    steps = groups // max(d for d in range(1, 15) if groups % d == 0)
    out = pl.pallas_call(
        functools.partial(attend_kernel, score_scale, steps, blocks),
        out_shape=[
            pltpu.VMEM((requests + 1, heads_here, latent_size), jnp.bfloat16)
            for _ in range(blocks)
        ]
        + [pltpu.VMEM(output_weight.shape, output_weight.dtype)],
        in_specs=[SMEM_SPEC, pl.BlockSpec(memory_space=pl.ANY)]
        + [VMEM_SPEC] * (CACHE_PARTS + blocks),
        out_specs=[VMEM_SPEC] * (blocks + 1),
        scratch_shapes=[
            pltpu.VMEM((requests, heads, entry_size), jnp.bfloat16),
            pltpu.VMEM((pages // 2, heads, pair_len), jnp.float32),
            pltpu.VMEM((requests + 1, heads, pair_len), jnp.float32),
            pltpu.VMEM((requests + 1, heads, pair_len), jnp.float32),
            pltpu.VMEM((requests + 1, heads, latent_size), jnp.float32),
            pltpu.SemaphoreType.DMA,
        ],
        compiler_params=pltpu.CompilerParams(vmem_limit_bytes=16 * MIB),
        cost_estimate=pl.CostEstimate(
            flops=2 * pages * page_len * heads * (entry_size + latent_size) * 4,
            bytes_accessed=pages * page_len * entry_size * 2,
            transcendentals=pages * page_len * heads,
        ),
        name="attend",
    )(page_owner, output_weight, *map(in_vmem, [*cache_parts, *query_blocks]))
    return list(out[:-1]), out[-1]


def shares(levels):
    top = functools.reduce(jnp.maximum, levels)
    parts = [jnp.exp(level - top) for level in levels]
    total = functools.reduce(jnp.add, parts)
    return [part / total for part in parts], top + jnp.log(total)


def merge_kernel(own_ref, got_ref, out_ref):
    requests = own_ref.shape[0] - 1
    both = (own_ref, got_ref)
    weights, level = shares([load_level(ref, requests) for ref in both])
    for r in range(requests):
        out_ref[r] = sum(
            w[:, r : r + 1] * ref[r].astype(jnp.float32) for w, ref in zip(weights, both)
        ).astype(jnp.bfloat16)
    out_ref[requests] = jnp.zeros(out_ref.shape[1:], jnp.bfloat16)
    store_level(out_ref, requests, level)


def merge(own, got):
    return pl.pallas_call(
        merge_kernel,
        out_shape=pltpu.VMEM(own.shape, own.dtype),
        in_specs=[VMEM_SPEC] * 2,
        out_specs=VMEM_SPEC,
        compiler_params=pltpu.CompilerParams(vmem_limit_bytes=2 * MIB),
        cost_estimate=pl.CostEstimate(flops=4 * own.size, bytes_accessed=0, transcendentals=0),
        name="merge",
    )(in_vmem(own), in_vmem(got))


def finish_kernel(
    block_columns, radices, here_ref, value_ref, weight_ref, *refs
):
    messages, (out_ref, attended_scr, head_scr) = refs[:-3], refs[-3:]
    requests, heads_here = messages[0].shape[0] - 1, messages[0].shape[1]
    value_size = value_ref.shape[2]
    owners, _, width = out_ref.shape
    weights, _ = shares([load_level(ref, requests) for ref in messages])
    for r in range(requests):
        attended_scr[r * heads_here : (r + 1) * heads_here] = sum(
            w[:, r : r + 1] * ref[r].astype(jnp.float32) for w, ref in zip(weights, messages)
        )
    attended = attended_scr[...].astype(jnp.bfloat16)
    row = lax.broadcasted_iota(jnp.int32, (requests, requests * heads_here), 0)
    column = lax.broadcasted_iota(jnp.int32, (requests, requests * heads_here), 1)
    for h in range(heads_here):
        pick = jnp.where(column == row * heads_here + h, 1.0, 0.0).astype(jnp.bfloat16)
        rows = jnp.dot(pick, attended, preferred_element_type=jnp.float32).astype(jnp.bfloat16)
        head_scr[:, h * value_size : (h + 1) * value_size] = jnp.dot(
            rows, value_ref[h], preferred_element_type=jnp.float32
        ).astype(jnp.bfloat16)
    head_out = head_scr[...]
    per_block = block_columns // width
    for j in range(owners // per_block):
        product = jnp.dot(
            head_out,
            weight_ref[:, j * block_columns : (j + 1) * block_columns],
            preferred_element_type=jnp.float32,
        ).astype(jnp.bfloat16)
        for i in range(per_block):
            distance = here_ref[0] ^ (j * per_block + i)
            place = 0
            for radix in radices:
                place = place * radix + (distance & (radix - 1))
                distance = distance >> (radix.bit_length() - 1)
            out_ref[place] = product[:, i * width : (i + 1) * width]


def finish(here, messages, value_absorb, weight, radices):
    requests, heads_here = messages[0].shape[0] - 1, messages[0].shape[1]
    latent_size, value_size = value_absorb.shape[1:]
    depth, columns = weight.shape
    owners = functools.reduce(lambda a, b: a * b, radices)
    width = columns // owners
    block_columns = width
    while block_columns % LANES:
        block_columns *= 2
    return pl.pallas_call(
        functools.partial(finish_kernel, block_columns, radices),
        out_shape=pltpu.VMEM((owners, requests, width), jnp.bfloat16),
        in_specs=[SMEM_SPEC] + [VMEM_SPEC] * (2 + len(messages)),
        out_specs=VMEM_SPEC,
        scratch_shapes=[
            pltpu.VMEM((requests * heads_here, latent_size), jnp.float32),
            pltpu.VMEM((requests, heads_here * value_size), jnp.bfloat16),
        ],
        compiler_params=pltpu.CompilerParams(vmem_limit_bytes=8 * MIB),
        cost_estimate=pl.CostEstimate(
            flops=2 * 256 * depth * columns, bytes_accessed=0, transcendentals=0
        ),
        name="finish",
    )(here, *[in_vmem(x) for x in (value_absorb, weight, *messages)])


def body(
    query_nope, query_rope, key_absorb, value_absorb, output_weight, latent_cache, page_owner
):
    requests, heads_here, nope_size = query_nope.shape
    latent_size = key_absorb.shape[2]
    rope_size = query_rope.shape[1] // heads_here
    score_scale = (nope_size + rope_size) ** (-0.5)
    count = lax.axis_size("ctx")
    axes = ("ctx", "head")
    here = lax.axis_index(axes).astype(jnp.int32).reshape(1)

    def exchange(x, distance):
        return lax.ppermute(x, "ctx", [(i, i ^ distance) for i in range(count)])

    query_latent = jnp.einsum(
        "rhn,hnl->rhl", query_nope, key_absorb, preferred_element_type=jnp.float32
    ).astype(jnp.bfloat16)
    ropes_row = latent_size // rope_size
    rope = query_rope.reshape(-1, ropes_row, heads_here, rope_size).transpose(0, 2, 1, 3)
    own = jnp.concatenate([query_latent, rope.reshape(-1, heads_here, latent_size)], axis=0)

    even = [*range(4, count, 2), *range(2, min(4, count), 2)]
    block_at = {distance: exchange(own, distance) for distance in [*even, 1]}
    cache_parts = [load(here, latent_cache, 0, CACHE_PARTS, own)]
    here, (block_at[2], block_at[1]) = gate(here, [block_at[2], block_at[1]], cache_parts[0])
    for part in range(1, CACHE_PARTS):
        cache_parts.append(load(here, latent_cache, part, CACHE_PARTS, block_at[2]))
    block_at[3] = exchange(block_at[2], 1)
    for distance in even[:-1]:
        _, (block_at[distance],) = gate(here, [block_at[distance]], cache_parts[-1])
        block_at[distance ^ 1] = exchange(block_at[distance], 1)
    block_at[0] = own

    message_to, weight = attend(
        [block_at[d] for d in range(count)],
        cache_parts, page_owner, output_weight, score_scale, latent_size,
    )

    across = {distance: exchange(message_to[distance ^ 1], 1) for distance in [*even, 0]}
    arrived = [
        exchange(merge(message_to[distance], across[distance]), distance) for distance in even
    ]
    messages = [message_to[0], across[0], *arrived]

    owners = lax.axis_size(axes)
    radices = [4] * ((owners.bit_length() - 1) // 2) + [2] * ((owners.bit_length() - 1) % 2)
    pieces = finish(here, messages, value_absorb, weight, radices)
    unit = 1
    for radix in radices:
        share = pieces.shape[0] // radix
        got = [
            lax.ppermute(
                pieces[k * share : (k + 1) * share],
                axes,
                [(i, i ^ (k * unit)) for i in range(owners)],
            )
            for k in range(1, radix)
        ]
        pieces = sum(x.astype(jnp.float32) for x in [pieces[:share], *got]).astype(jnp.bfloat16)
        unit *= radix
    return pieces[0]


def solution(mesh):
    return jax.shard_map(
        body,
        mesh=mesh,
        in_specs=(
            P("groups", ("ctx", "head"), None),
            P("groups", ("ctx", "head")),
            P(("ctx", "head"), None, None),
            P(("ctx", "head"), None, None),
            P(("ctx", "head"), None),
            P(("groups", "ctx"), None, None),
            P(("groups", "ctx")),
        ),
        out_specs=P("groups", ("ctx", "head")),
        check_vma=False,
    )
```

```python
import functools

import jax
import jax.numpy as jnp
from jax import lax
from jax.experimental import pallas as pl
from jax.experimental.pallas import tpu as pltpu
from jax.sharding import PartitionSpec as P

masked_score = -1e30
LANES = 128
GROUP_PAGES = 4
CACHE_PARTS = 2
MIB = 1024 * 1024

VMEM_SPEC = pl.BlockSpec(memory_space=pltpu.VMEM)
SMEM_SPEC = pl.BlockSpec(memory_space=pltpu.SMEM)


def in_vmem(x):
    return pltpu.with_memory_space_constraint(x, pltpu.VMEM)


def split_level(level):
    high = level.astype(jnp.bfloat16)
    rest = level - high.astype(jnp.float32)
    middle = rest.astype(jnp.bfloat16)
    low = (rest - middle.astype(jnp.float32)).astype(jnp.bfloat16)
    return high, middle, low


def store_level(message_ref, row, level):
    for i, part in enumerate(split_level(level)):
        message_ref[row, :, i * LANES : (i + 1) * LANES] = part


def load_level(message_ref, row):
    parts = [
        message_ref[row, :, i * LANES : (i + 1) * LANES].astype(jnp.float32) for i in range(3)
    ]
    return (parts[0] + parts[1]) + parts[2]


def load_kernel(first, here_ref, cache_ref, after_ref, out_ref, sem):
    copy = pltpu.make_async_copy(cache_ref.at[pl.ds(first, out_ref.shape[0])], out_ref, sem)
    copy.start()
    copy.wait()


def load(here, cache, part, parts, after):
    pages = cache.shape[0] // parts
    return pl.pallas_call(
        functools.partial(load_kernel, part * pages),
        out_shape=pltpu.VMEM((pages, *cache.shape[1:]), cache.dtype),
        in_specs=[
            SMEM_SPEC,
            pl.BlockSpec(memory_space=pltpu.HBM),
            pl.BlockSpec(memory_space=pl.ANY),
        ],
        out_specs=VMEM_SPEC,
        scratch_shapes=[pltpu.SemaphoreType.DMA],
        compiler_params=pltpu.CompilerParams(vmem_limit_bytes=MIB),
        cost_estimate=pl.CostEstimate(
            flops=0, bytes_accessed=2 * cache.size // parts, transcendentals=0
        ),
        name="load",
    )(here, pltpu.with_memory_space_constraint(cache, pltpu.HBM), after)


def gate_kernel(block_ref, after_ref, out_ref):
    pass


def gate(block, after):
    return pl.pallas_call(
        gate_kernel,
        out_shape=jax.ShapeDtypeStruct(block.shape, block.dtype),
        in_specs=[pl.BlockSpec(memory_space=pl.ANY)] * 2,
        out_specs=pl.BlockSpec(memory_space=pl.ANY),
        input_output_aliases={0: 0},
        compiler_params=pltpu.CompilerParams(vmem_limit_bytes=MIB),
        cost_estimate=pl.CostEstimate(flops=0, bytes_accessed=0, transcendentals=0),
        name="gate",
    )(block, after)


def attend_kernel(score_scale, steps, blocks, owner_ref, weight_ref, *refs):
    cache_refs, refs = refs[:CACHE_PARTS], refs[CACHE_PARTS:]
    query_refs, message_refs = refs[:blocks], refs[blocks : 2 * blocks]
    weight_out, query_scr, score_scr, max_scr, total_scr, sum_scr, weight_sem = refs[2 * blocks :]
    requests, heads, entry_size = query_scr.shape
    pages_part, page_len, _ = cache_refs[0].shape
    _, heads_here, latent_size = message_refs[0].shape
    rope_size = entry_size - latent_size
    ropes_row = latent_size // rope_size
    pair_len = 2 * page_len
    pair_count = GROUP_PAGES // 2
    groups_part = pages_part // GROUP_PAGES
    groups_step = groups_part // steps
    group_len = GROUP_PAGES * page_len

    weight_copy = pltpu.make_async_copy(weight_ref, weight_out, weight_sem)
    weight_copy.start()

    for b, ref in enumerate(query_refs):
        rows = slice(b * heads_here, (b + 1) * heads_here)
        for r in range(requests):
            start = r % ropes_row * rope_size
            query_scr[r, rows, :latent_size] = ref[r]
            query_scr[r, rows, latent_size:] = ref[requests + r // ropes_row][
                :, start : start + rope_size
            ]

    first_half = lax.broadcasted_iota(jnp.int32, (heads, pair_len), 1) < page_len

    for r in range(requests + 1):
        max_scr[r] = jnp.full((heads, pair_len), masked_score, jnp.float32)
        total_scr[r] = jnp.zeros((heads, pair_len), jnp.float32)
        sum_scr[r] = jnp.zeros((heads, latent_size), jnp.float32)

    def owners_of(g):
        raw = [owner_ref[g * GROUP_PAGES + k] for k in range(GROUP_PAGES)]
        return [jnp.where(o < 0, requests, o) for o in raw]

    def score_group(part, local):
        g = part * groups_part + local
        owners = owners_of(g)
        keys = cache_refs[part][pl.ds(local * GROUP_PAGES, GROUP_PAGES)].reshape(group_len, entry_size)
        queries = jnp.concatenate(
            [query_scr[jnp.minimum(o, requests - 1)] for o in owners], axis=0
        )
        scores = lax.dot_general(
            queries, keys, (((1,), (1,)), ((), ())), preferred_element_type=jnp.float32
        )
        for p in range(pair_count):
            left, right = 2 * p, 2 * p + 1
            columns = slice(p * pair_len, (p + 1) * pair_len)
            pair = score_scale * jnp.where(
                first_half,
                scores[left * heads : (left + 1) * heads, columns],
                scores[right * heads : (right + 1) * heads, columns],
            )
            score_scr[g * pair_count + p] = pair
            max_scr[owners[left]] = jnp.maximum(
                max_scr[owners[left]], jnp.where(first_half, pair, masked_score)
            )
            max_scr[owners[right]] = jnp.maximum(
                max_scr[owners[right]], jnp.where(first_half, masked_score, pair)
            )

    def score_step(part, c, carry):
        for i in range(groups_step):
            score_group(part, c * groups_step + i)
        return carry

    for part in range(CACHE_PARTS):
        lax.fori_loop(0, steps, functools.partial(score_step, part), 0)

    for r in range(requests + 1):
        top = jnp.max(max_scr[r], axis=1, keepdims=True)
        max_scr[r] = jnp.broadcast_to(top, (heads, pair_len))

    def sum_group(part, local):
        g = part * groups_part + local
        owners = owners_of(g)
        values = cache_refs[part][pl.ds(local * GROUP_PAGES, GROUP_PAGES)].reshape(group_len, entry_size)[
            :, :latent_size
        ]
        rows = []
        for p in range(pair_count):
            left, right = owners[2 * p], owners[2 * p + 1]
            offset = jnp.where(first_half, max_scr[left], max_scr[right])
            weight = jnp.exp(score_scr[g * pair_count + p] - offset)
            left_weight = jnp.where(first_half, weight, 0.0)
            right_weight = jnp.where(first_half, 0.0, weight)
            total_scr[left] += left_weight
            total_scr[right] += right_weight
            for part in (left_weight, right_weight):
                half = part.astype(jnp.bfloat16)
                pieces = [half if q == p else jnp.zeros_like(half) for q in range(pair_count)]
                rows.append(jnp.concatenate(pieces, axis=1))
        added = jnp.dot(
            jnp.concatenate(rows, axis=0), values, preferred_element_type=jnp.float32
        )
        for k in range(GROUP_PAGES):
            sum_scr[owners[k]] += added[k * heads : (k + 1) * heads]

    def sum_step(part, c, carry):
        for i in range(groups_step):
            sum_group(part, c * groups_step + i)
        return carry

    for part in range(CACHE_PARTS):
        lax.fori_loop(0, steps, functools.partial(sum_step, part), 0)

    lane = lax.broadcasted_iota(jnp.int32, (heads, LANES), 1)
    stats = jnp.full((heads, LANES), masked_score, jnp.float32)
    for r in range(requests):
        total = jnp.sum(total_scr[r], axis=1, keepdims=True)
        present = total > 0.0
        safe = jnp.where(present, total, 1.0)
        mean = (sum_scr[r] * (1.0 / safe)).astype(jnp.bfloat16)
        level = jnp.where(present, max_scr[r][:, :1] + jnp.log(safe), masked_score)
        stats = jnp.where(lane == r, level, stats)
        for b in range(blocks):
            message_refs[b][r] = mean[b * heads_here : (b + 1) * heads_here]
    for b in range(blocks):
        message_refs[b][requests] = jnp.zeros((heads_here, latent_size), jnp.bfloat16)
        store_level(message_refs[b], requests, stats[b * heads_here : (b + 1) * heads_here])
    weight_copy.wait()


def attend(query_blocks, cache_parts, page_owner, output_weight, score_scale, latent_size):
    pages_part, page_len, entry_size = cache_parts[0].shape
    pages = pages_part * CACHE_PARTS
    blocks = len(query_blocks)
    heads_here = query_blocks[0].shape[1]
    requests = query_blocks[0].shape[0] * latent_size // entry_size
    heads = heads_here * blocks
    pair_len = 2 * page_len
    groups = pages_part // GROUP_PAGES
    steps = groups // max(d for d in range(1, 15) if groups % d == 0)
    out = pl.pallas_call(
        functools.partial(attend_kernel, score_scale, steps, blocks),
        out_shape=[
            pltpu.VMEM((requests + 1, heads_here, latent_size), jnp.bfloat16)
            for _ in range(blocks)
        ]
        + [pltpu.VMEM(output_weight.shape, output_weight.dtype)],
        in_specs=[SMEM_SPEC, pl.BlockSpec(memory_space=pl.ANY)]
        + [VMEM_SPEC] * (CACHE_PARTS + blocks),
        out_specs=[VMEM_SPEC] * (blocks + 1),
        scratch_shapes=[
            pltpu.VMEM((requests, heads, entry_size), jnp.bfloat16),
            pltpu.VMEM((pages // 2, heads, pair_len), jnp.float32),
            pltpu.VMEM((requests + 1, heads, pair_len), jnp.float32),
            pltpu.VMEM((requests + 1, heads, pair_len), jnp.float32),
            pltpu.VMEM((requests + 1, heads, latent_size), jnp.float32),
            pltpu.SemaphoreType.DMA,
        ],
        compiler_params=pltpu.CompilerParams(vmem_limit_bytes=16 * MIB),
        cost_estimate=pl.CostEstimate(
            flops=2 * pages * page_len * heads * (entry_size + latent_size) * 4,
            bytes_accessed=pages * page_len * entry_size * 2,
            transcendentals=pages * page_len * heads,
        ),
        name="attend",
    )(page_owner, output_weight, *map(in_vmem, [*cache_parts, *query_blocks]))
    return list(out[:-1]), out[-1]


def shares(levels):
    top = functools.reduce(jnp.maximum, levels)
    parts = [jnp.exp(level - top) for level in levels]
    total = functools.reduce(jnp.add, parts)
    return [part / total for part in parts], top + jnp.log(total)


def merge_kernel(own_ref, got_ref, out_ref):
    requests = own_ref.shape[0] - 1
    both = (own_ref, got_ref)
    weights, level = shares([load_level(ref, requests) for ref in both])
    for r in range(requests):
        out_ref[r] = sum(
            w[:, r : r + 1] * ref[r].astype(jnp.float32) for w, ref in zip(weights, both)
        ).astype(jnp.bfloat16)
    out_ref[requests] = jnp.zeros(out_ref.shape[1:], jnp.bfloat16)
    store_level(out_ref, requests, level)


def merge(own, got):
    return pl.pallas_call(
        merge_kernel,
        out_shape=pltpu.VMEM(own.shape, own.dtype),
        in_specs=[VMEM_SPEC] * 2,
        out_specs=VMEM_SPEC,
        compiler_params=pltpu.CompilerParams(vmem_limit_bytes=2 * MIB),
        cost_estimate=pl.CostEstimate(flops=4 * own.size, bytes_accessed=0, transcendentals=0),
        name="merge",
    )(in_vmem(own), in_vmem(got))


def finish_kernel(
    block_columns, count, here_ref, value_ref, weight_ref, *refs
):
    messages, (out_ref, attended_scr, head_scr) = refs[:-3], refs[-3:]
    requests, heads_here = messages[0].shape[0] - 1, messages[0].shape[1]
    value_size = value_ref.shape[2]
    owners, _, width = out_ref.shape
    weights, _ = shares([load_level(ref, requests) for ref in messages])
    for r in range(requests):
        attended_scr[r * heads_here : (r + 1) * heads_here] = sum(
            w[:, r : r + 1] * ref[r].astype(jnp.float32) for w, ref in zip(weights, messages)
        )
    attended = attended_scr[...].astype(jnp.bfloat16)
    row = lax.broadcasted_iota(jnp.int32, (requests, requests * heads_here), 0)
    column = lax.broadcasted_iota(jnp.int32, (requests, requests * heads_here), 1)
    for h in range(heads_here):
        pick = jnp.where(column == row * heads_here + h, 1.0, 0.0).astype(jnp.bfloat16)
        rows = jnp.dot(pick, attended, preferred_element_type=jnp.float32).astype(jnp.bfloat16)
        head_scr[:, h * value_size : (h + 1) * value_size] = jnp.dot(
            rows, value_ref[h], preferred_element_type=jnp.float32
        ).astype(jnp.bfloat16)
    head_out = head_scr[...]
    per_block = block_columns // width
    for j in range(owners // per_block):
        product = jnp.dot(
            head_out,
            weight_ref[:, j * block_columns : (j + 1) * block_columns],
            preferred_element_type=jnp.float32,
        ).astype(jnp.bfloat16)
        for i in range(per_block):
            ctx, head = divmod(j * per_block + i, owners // count)
            place = (here_ref[0] ^ head) * count + ctx
            out_ref[place] = product[:, i * width : (i + 1) * width]


def finish(here, messages, value_absorb, weight, count, owners):
    requests, heads_here = messages[0].shape[0] - 1, messages[0].shape[1]
    latent_size, value_size = value_absorb.shape[1:]
    depth, columns = weight.shape
    width = columns // owners
    block_columns = width
    while block_columns % LANES:
        block_columns *= 2
    return pl.pallas_call(
        functools.partial(finish_kernel, block_columns, count),
        out_shape=pltpu.VMEM((owners, requests, width), jnp.bfloat16),
        in_specs=[SMEM_SPEC] + [VMEM_SPEC] * (2 + len(messages)),
        out_specs=VMEM_SPEC,
        scratch_shapes=[
            pltpu.VMEM((requests * heads_here, latent_size), jnp.float32),
            pltpu.VMEM((requests, heads_here * value_size), jnp.bfloat16),
        ],
        compiler_params=pltpu.CompilerParams(vmem_limit_bytes=8 * MIB),
        cost_estimate=pl.CostEstimate(
            flops=2 * 256 * depth * columns, bytes_accessed=0, transcendentals=0
        ),
        name="finish",
    )(here, *[in_vmem(x) for x in (value_absorb, weight, *messages)])


def body(
    query_nope, query_rope, key_absorb, value_absorb, output_weight, latent_cache, page_owner
):
    requests, heads_here, nope_size = query_nope.shape
    latent_size = key_absorb.shape[2]
    rope_size = query_rope.shape[1] // heads_here
    score_scale = (nope_size + rope_size) ** (-0.5)
    count = lax.axis_size("ctx")
    cores = lax.axis_size("head")
    here = lax.axis_index("head").astype(jnp.int32).reshape(1)

    def exchange(x, distance):
        return lax.ppermute(x, "ctx", [(i, i ^ distance) for i in range(count)])

    query_latent = jnp.einsum(
        "rhn,hnl->rhl", query_nope, key_absorb, preferred_element_type=jnp.float32
    ).astype(jnp.bfloat16)
    ropes_row = latent_size // rope_size
    rope = query_rope.reshape(-1, ropes_row, heads_here, rope_size).transpose(0, 2, 1, 3)
    own = jnp.concatenate([query_latent, rope.reshape(-1, heads_here, latent_size)], axis=0)

    even = [*range(4, count, 2), *range(2, min(4, count), 2)]
    block_at = {distance: exchange(own, distance) for distance in [*even, 3, 1]}
    block_at[0] = own
    cache_parts, last = [], own
    for part in range(CACHE_PARTS):
        last = load(here, latent_cache, part, CACHE_PARTS, last)
        cache_parts.append(last)
    for distance in even[:-1]:
        block_at[distance] = gate(block_at[distance], last)
        block_at[distance ^ 1] = exchange(block_at[distance], 1)

    message_to, weight = attend(
        [block_at[d] for d in range(count)],
        cache_parts, page_owner, output_weight, score_scale, latent_size,
    )

    across = {distance: exchange(message_to[distance ^ 1], 1) for distance in [*even, 0]}
    arrived = [
        exchange(merge(message_to[distance], across[distance]), distance) for distance in even
    ]
    messages = [message_to[0], across[0], *arrived]

    pieces = finish(here, messages, value_absorb, weight, count, count * cores)
    total = pieces[:count].astype(jnp.float32)
    for distance in range(1, cores):
        got = lax.ppermute(
            pieces[distance * count : (distance + 1) * count],
            "head",
            [(i, i ^ distance) for i in range(cores)],
        )
        total = total + got.astype(jnp.float32)
    pieces = lax.all_to_all(
        total.astype(jnp.bfloat16), "ctx", split_axis=0, concat_axis=0, tiled=True
    )
    return jnp.sum(pieces.astype(jnp.float32), axis=0).astype(jnp.bfloat16)


def solution(mesh):
    return jax.shard_map(
        body,
        mesh=mesh,
        in_specs=(
            P("groups", ("ctx", "head"), None),
            P("groups", ("ctx", "head")),
            P(("ctx", "head"), None, None),
            P(("ctx", "head"), None, None),
            P(("ctx", "head"), None),
            P(("groups", "ctx"), None, None),
            P(("groups", "ctx")),
        ),
        out_specs=P("groups", ("ctx", "head")),
        check_vma=False,
    )
```

```python
import functools

import jax
import jax.numpy as jnp
from jax import lax
from jax.experimental import pallas as pl
from jax.experimental.pallas import tpu as pltpu
from jax.sharding import PartitionSpec as P

masked_score = -1e30
LANES = 128
GROUP_PAGES = 4
CACHE_PARTS = 2
MIB = 1024 * 1024

VMEM_SPEC = pl.BlockSpec(memory_space=pltpu.VMEM)
SMEM_SPEC = pl.BlockSpec(memory_space=pltpu.SMEM)


def in_vmem(x):
    return pltpu.with_memory_space_constraint(x, pltpu.VMEM)


def split_level(level):
    high = level.astype(jnp.bfloat16)
    rest = level - high.astype(jnp.float32)
    middle = rest.astype(jnp.bfloat16)
    low = (rest - middle.astype(jnp.float32)).astype(jnp.bfloat16)
    return high, middle, low


def store_level(message_ref, row, level):
    for i, part in enumerate(split_level(level)):
        message_ref[row, :, i * LANES : (i + 1) * LANES] = part


def load_level(message_ref, row):
    parts = [
        message_ref[row, :, i * LANES : (i + 1) * LANES].astype(jnp.float32) for i in range(3)
    ]
    return (parts[0] + parts[1]) + parts[2]


def load_kernel(first, here_ref, cache_ref, after_ref, out_ref, sem):
    copy = pltpu.make_async_copy(cache_ref.at[pl.ds(first, out_ref.shape[0])], out_ref, sem)
    copy.start()
    copy.wait()


def load(here, cache, part, parts, after):
    pages = cache.shape[0] // parts
    return pl.pallas_call(
        functools.partial(load_kernel, part * pages),
        out_shape=pltpu.VMEM((pages, *cache.shape[1:]), cache.dtype),
        in_specs=[
            SMEM_SPEC,
            pl.BlockSpec(memory_space=pltpu.HBM),
            pl.BlockSpec(memory_space=pl.ANY),
        ],
        out_specs=VMEM_SPEC,
        scratch_shapes=[pltpu.SemaphoreType.DMA],
        compiler_params=pltpu.CompilerParams(vmem_limit_bytes=MIB),
        cost_estimate=pl.CostEstimate(
            flops=0, bytes_accessed=2 * cache.size // parts, transcendentals=0
        ),
        name="load",
    )(here, pltpu.with_memory_space_constraint(cache, pltpu.HBM), after)


def gate_kernel(block_ref, after_ref, out_ref):
    pass


def gate(block, after):
    return pl.pallas_call(
        gate_kernel,
        out_shape=jax.ShapeDtypeStruct(block.shape, block.dtype),
        in_specs=[pl.BlockSpec(memory_space=pl.ANY)] * 2,
        out_specs=pl.BlockSpec(memory_space=pl.ANY),
        input_output_aliases={0: 0},
        compiler_params=pltpu.CompilerParams(vmem_limit_bytes=MIB),
        cost_estimate=pl.CostEstimate(flops=0, bytes_accessed=0, transcendentals=0),
        name="gate",
    )(block, after)


def attend_kernel(score_scale, steps, blocks, owner_ref, weight_ref, *refs):
    cache_refs, refs = refs[:CACHE_PARTS], refs[CACHE_PARTS:]
    query_refs, message_refs = refs[:blocks], refs[blocks : 2 * blocks]
    weight_out, query_scr, score_scr, max_scr, total_scr, sum_scr, weight_sem = refs[2 * blocks :]
    requests, heads, entry_size = query_scr.shape
    pages_part, page_len, _ = cache_refs[0].shape
    _, heads_here, latent_size = message_refs[0].shape
    rope_size = entry_size - latent_size
    ropes_row = latent_size // rope_size
    pair_len = 2 * page_len
    pair_count = GROUP_PAGES // 2
    groups_part = pages_part // GROUP_PAGES
    groups_step = groups_part // steps
    group_len = GROUP_PAGES * page_len

    weight_copy = pltpu.make_async_copy(weight_ref, weight_out, weight_sem)
    weight_copy.start()

    for b, ref in enumerate(query_refs):
        rows = slice(b * heads_here, (b + 1) * heads_here)
        for r in range(requests):
            start = r % ropes_row * rope_size
            query_scr[r, rows, :latent_size] = ref[r]
            query_scr[r, rows, latent_size:] = ref[requests + r // ropes_row][
                :, start : start + rope_size
            ]

    first_half = lax.broadcasted_iota(jnp.int32, (heads, pair_len), 1) < page_len

    for r in range(requests + 1):
        max_scr[r] = jnp.full((heads, pair_len), masked_score, jnp.float32)
        total_scr[r] = jnp.zeros((heads, pair_len), jnp.float32)
        sum_scr[r] = jnp.zeros((heads, latent_size), jnp.float32)

    def owners_of(g):
        raw = [owner_ref[g * GROUP_PAGES + k] for k in range(GROUP_PAGES)]
        return [jnp.where(o < 0, requests, o) for o in raw]

    def score_group(part, local):
        g = part * groups_part + local
        owners = owners_of(g)
        keys = cache_refs[part][pl.ds(local * GROUP_PAGES, GROUP_PAGES)].reshape(group_len, entry_size)
        queries = jnp.concatenate(
            [query_scr[jnp.minimum(o, requests - 1)] for o in owners], axis=0
        )
        scores = lax.dot_general(
            queries, keys, (((1,), (1,)), ((), ())), preferred_element_type=jnp.float32
        )
        for p in range(pair_count):
            left, right = 2 * p, 2 * p + 1
            columns = slice(p * pair_len, (p + 1) * pair_len)
            pair = score_scale * jnp.where(
                first_half,
                scores[left * heads : (left + 1) * heads, columns],
                scores[right * heads : (right + 1) * heads, columns],
            )
            score_scr[g * pair_count + p] = pair
            max_scr[owners[left]] = jnp.maximum(
                max_scr[owners[left]], jnp.where(first_half, pair, masked_score)
            )
            max_scr[owners[right]] = jnp.maximum(
                max_scr[owners[right]], jnp.where(first_half, masked_score, pair)
            )

    def score_step(part, c, carry):
        for i in range(groups_step):
            score_group(part, c * groups_step + i)
        return carry

    for part in range(CACHE_PARTS):
        lax.fori_loop(0, steps, functools.partial(score_step, part), 0)

    for r in range(requests + 1):
        top = jnp.max(max_scr[r], axis=1, keepdims=True)
        max_scr[r] = jnp.broadcast_to(top, (heads, pair_len))

    def sum_group(part, local):
        g = part * groups_part + local
        owners = owners_of(g)
        values = cache_refs[part][pl.ds(local * GROUP_PAGES, GROUP_PAGES)].reshape(group_len, entry_size)[
            :, :latent_size
        ]
        rows = []
        for p in range(pair_count):
            left, right = owners[2 * p], owners[2 * p + 1]
            offset = jnp.where(first_half, max_scr[left], max_scr[right])
            weight = jnp.exp(score_scr[g * pair_count + p] - offset)
            left_weight = jnp.where(first_half, weight, 0.0)
            right_weight = jnp.where(first_half, 0.0, weight)
            total_scr[left] += left_weight
            total_scr[right] += right_weight
            for part in (left_weight, right_weight):
                half = part.astype(jnp.bfloat16)
                pieces = [half if q == p else jnp.zeros_like(half) for q in range(pair_count)]
                rows.append(jnp.concatenate(pieces, axis=1))
        added = jnp.dot(
            jnp.concatenate(rows, axis=0), values, preferred_element_type=jnp.float32
        )
        for k in range(GROUP_PAGES):
            sum_scr[owners[k]] += added[k * heads : (k + 1) * heads]

    def sum_step(part, c, carry):
        for i in range(groups_step):
            sum_group(part, c * groups_step + i)
        return carry

    for part in range(CACHE_PARTS):
        lax.fori_loop(0, steps, functools.partial(sum_step, part), 0)

    lane = lax.broadcasted_iota(jnp.int32, (heads, LANES), 1)
    stats = jnp.full((heads, LANES), masked_score, jnp.float32)
    for r in range(requests):
        total = jnp.sum(total_scr[r], axis=1, keepdims=True)
        present = total > 0.0
        safe = jnp.where(present, total, 1.0)
        mean = (sum_scr[r] * (1.0 / safe)).astype(jnp.bfloat16)
        level = jnp.where(present, max_scr[r][:, :1] + jnp.log(safe), masked_score)
        stats = jnp.where(lane == r, level, stats)
        for b in range(blocks):
            message_refs[b][r] = mean[b * heads_here : (b + 1) * heads_here]
    for b in range(blocks):
        message_refs[b][requests] = jnp.zeros((heads_here, latent_size), jnp.bfloat16)
        store_level(message_refs[b], requests, stats[b * heads_here : (b + 1) * heads_here])
    weight_copy.wait()


def attend(query_blocks, cache_parts, page_owner, output_weight, score_scale, latent_size):
    pages_part, page_len, entry_size = cache_parts[0].shape
    pages = pages_part * CACHE_PARTS
    blocks = len(query_blocks)
    heads_here = query_blocks[0].shape[1]
    requests = query_blocks[0].shape[0] * latent_size // entry_size
    heads = heads_here * blocks
    pair_len = 2 * page_len
    groups = pages_part // GROUP_PAGES
    steps = groups // max(d for d in range(1, 15) if groups % d == 0)
    out = pl.pallas_call(
        functools.partial(attend_kernel, score_scale, steps, blocks),
        out_shape=[
            pltpu.VMEM((requests + 1, heads_here, latent_size), jnp.bfloat16)
            for _ in range(blocks)
        ]
        + [pltpu.VMEM(output_weight.shape, output_weight.dtype)],
        in_specs=[SMEM_SPEC, pl.BlockSpec(memory_space=pl.ANY)]
        + [VMEM_SPEC] * (CACHE_PARTS + blocks),
        out_specs=[VMEM_SPEC] * (blocks + 1),
        scratch_shapes=[
            pltpu.VMEM((requests, heads, entry_size), jnp.bfloat16),
            pltpu.VMEM((pages // 2, heads, pair_len), jnp.float32),
            pltpu.VMEM((requests + 1, heads, pair_len), jnp.float32),
            pltpu.VMEM((requests + 1, heads, pair_len), jnp.float32),
            pltpu.VMEM((requests + 1, heads, latent_size), jnp.float32),
            pltpu.SemaphoreType.DMA,
        ],
        compiler_params=pltpu.CompilerParams(vmem_limit_bytes=16 * MIB),
        cost_estimate=pl.CostEstimate(
            flops=2 * pages * page_len * heads * (entry_size + latent_size) * 4,
            bytes_accessed=pages * page_len * entry_size * 2,
            transcendentals=pages * page_len * heads,
        ),
        name="attend",
    )(page_owner, output_weight, *map(in_vmem, [*cache_parts, *query_blocks]))
    return list(out[:-1]), out[-1]


def shares(levels):
    top = functools.reduce(jnp.maximum, levels)
    parts = [jnp.exp(level - top) for level in levels]
    total = functools.reduce(jnp.add, parts)
    return [part / total for part in parts], top + jnp.log(total)


def merge_kernel(own_ref, got_ref, out_ref):
    requests = own_ref.shape[0] - 1
    both = (own_ref, got_ref)
    weights, level = shares([load_level(ref, requests) for ref in both])
    for r in range(requests):
        out_ref[r] = sum(
            w[:, r : r + 1] * ref[r].astype(jnp.float32) for w, ref in zip(weights, both)
        ).astype(jnp.bfloat16)
    out_ref[requests] = jnp.zeros(out_ref.shape[1:], jnp.bfloat16)
    store_level(out_ref, requests, level)


def merge(own, got):
    return pl.pallas_call(
        merge_kernel,
        out_shape=pltpu.VMEM(own.shape, own.dtype),
        in_specs=[VMEM_SPEC] * 2,
        out_specs=VMEM_SPEC,
        compiler_params=pltpu.CompilerParams(vmem_limit_bytes=2 * MIB),
        cost_estimate=pl.CostEstimate(flops=4 * own.size, bytes_accessed=0, transcendentals=0),
        name="merge",
    )(in_vmem(own), in_vmem(got))


def finish_kernel(
    block_columns, count, here_ref, value_ref, weight_ref, *refs
):
    messages, (out_ref, attended_scr, head_scr) = refs[:-3], refs[-3:]
    requests, heads_here = messages[0].shape[0] - 1, messages[0].shape[1]
    value_size = value_ref.shape[2]
    owners, _, width = out_ref.shape
    weights, _ = shares([load_level(ref, requests) for ref in messages])
    for r in range(requests):
        attended_scr[r * heads_here : (r + 1) * heads_here] = sum(
            w[:, r : r + 1] * ref[r].astype(jnp.float32) for w, ref in zip(weights, messages)
        )
    attended = attended_scr[...].astype(jnp.bfloat16)
    row = lax.broadcasted_iota(jnp.int32, (requests, requests * heads_here), 0)
    column = lax.broadcasted_iota(jnp.int32, (requests, requests * heads_here), 1)
    for h in range(heads_here):
        pick = jnp.where(column == row * heads_here + h, 1.0, 0.0).astype(jnp.bfloat16)
        rows = jnp.dot(pick, attended, preferred_element_type=jnp.float32).astype(jnp.bfloat16)
        head_scr[:, h * value_size : (h + 1) * value_size] = jnp.dot(
            rows, value_ref[h], preferred_element_type=jnp.float32
        ).astype(jnp.bfloat16)
    head_out = head_scr[...]
    per_block = block_columns // width
    for j in range(owners // per_block):
        product = jnp.dot(
            head_out,
            weight_ref[:, j * block_columns : (j + 1) * block_columns],
            preferred_element_type=jnp.float32,
        ).astype(jnp.bfloat16)
        for i in range(per_block):
            ctx, head = divmod(j * per_block + i, owners // count)
            place = (here_ref[0] ^ head) * count + ctx
            out_ref[place] = product[:, i * width : (i + 1) * width]


def finish(here, messages, value_absorb, weight, count, owners):
    requests, heads_here = messages[0].shape[0] - 1, messages[0].shape[1]
    latent_size, value_size = value_absorb.shape[1:]
    depth, columns = weight.shape
    width = columns // owners
    block_columns = width
    while block_columns % LANES:
        block_columns *= 2
    return pl.pallas_call(
        functools.partial(finish_kernel, block_columns, count),
        out_shape=pltpu.VMEM((owners, requests, width), jnp.bfloat16),
        in_specs=[SMEM_SPEC] + [VMEM_SPEC] * (2 + len(messages)),
        out_specs=VMEM_SPEC,
        scratch_shapes=[
            pltpu.VMEM((requests * heads_here, latent_size), jnp.float32),
            pltpu.VMEM((requests, heads_here * value_size), jnp.bfloat16),
        ],
        compiler_params=pltpu.CompilerParams(vmem_limit_bytes=8 * MIB),
        cost_estimate=pl.CostEstimate(
            flops=2 * 256 * depth * columns, bytes_accessed=0, transcendentals=0
        ),
        name="finish",
    )(here, *[in_vmem(x) for x in (value_absorb, weight, *messages)])


def body(
    query_nope, query_rope, key_absorb, value_absorb, output_weight, latent_cache, page_owner
):
    requests, heads_here, nope_size = query_nope.shape
    latent_size = key_absorb.shape[2]
    rope_size = query_rope.shape[1] // heads_here
    score_scale = (nope_size + rope_size) ** (-0.5)
    count = lax.axis_size("ctx")
    cores = lax.axis_size("head")
    here = lax.axis_index("head").astype(jnp.int32).reshape(1)

    def exchange(x, distance):
        return lax.ppermute(x, "ctx", [(i, i ^ distance) for i in range(count)])

    query_latent = jnp.einsum(
        "rhn,hnl->rhl", query_nope, key_absorb, preferred_element_type=jnp.float32
    ).astype(jnp.bfloat16)
    ropes_row = latent_size // rope_size
    rope = query_rope.reshape(-1, ropes_row, heads_here, rope_size).transpose(0, 2, 1, 3)
    own = jnp.concatenate([query_latent, rope.reshape(-1, heads_here, latent_size)], axis=0)

    even = [*range(4, count, 2), *range(2, min(4, count), 2)]
    block_at = {distance: exchange(own, distance) for distance in [*even, 3, 1]}
    block_at[0] = own
    cache_parts = [load(here, latent_cache, 0, CACHE_PARTS, own)]
    for distance in even[:-1]:
        block_at[distance] = gate(block_at[distance], cache_parts[0])
        block_at[distance ^ 1] = exchange(block_at[distance], 1)
    for part in range(1, CACHE_PARTS):
        cache_parts.append(load(here, latent_cache, part, CACHE_PARTS, block_at[count - 2]))

    message_to, weight = attend(
        [block_at[d] for d in range(count)],
        cache_parts, page_owner, output_weight, score_scale, latent_size,
    )

    across = {distance: exchange(message_to[distance ^ 1], 1) for distance in [*even, 0]}
    arrived = [
        exchange(merge(message_to[distance], across[distance]), distance) for distance in even
    ]
    messages = [message_to[0], across[0], *arrived]

    pieces = finish(here, messages, value_absorb, weight, count, count * cores)
    total = pieces[:count].astype(jnp.float32)
    for distance in range(1, cores):
        got = lax.ppermute(
            pieces[distance * count : (distance + 1) * count],
            "head",
            [(i, i ^ distance) for i in range(cores)],
        )
        total = total + got.astype(jnp.float32)
    pieces = lax.all_to_all(
        total.astype(jnp.bfloat16), "ctx", split_axis=0, concat_axis=0, tiled=True
    )
    return jnp.sum(pieces.astype(jnp.float32), axis=0).astype(jnp.bfloat16)


def solution(mesh):
    return jax.shard_map(
        body,
        mesh=mesh,
        in_specs=(
            P("groups", ("ctx", "head"), None),
            P("groups", ("ctx", "head")),
            P(("ctx", "head"), None, None),
            P(("ctx", "head"), None, None),
            P(("ctx", "head"), None),
            P(("groups", "ctx"), None, None),
            P(("groups", "ctx")),
        ),
        out_specs=P("groups", ("ctx", "head")),
        check_vma=False,
    )
```

```python
import functools

import jax
import jax.numpy as jnp
from jax import lax
from jax.experimental import pallas as pl
from jax.experimental.pallas import tpu as pltpu
from jax.sharding import PartitionSpec as P

masked_score = -1e30
LANES = 128
GROUP_PAGES = 4
CACHE_PARTS = 2
MIB = 1024 * 1024

VMEM_SPEC = pl.BlockSpec(memory_space=pltpu.VMEM)
SMEM_SPEC = pl.BlockSpec(memory_space=pltpu.SMEM)


def in_vmem(x):
    return pltpu.with_memory_space_constraint(x, pltpu.VMEM)


def split_level(level):
    high = level.astype(jnp.bfloat16)
    rest = level - high.astype(jnp.float32)
    middle = rest.astype(jnp.bfloat16)
    low = (rest - middle.astype(jnp.float32)).astype(jnp.bfloat16)
    return high, middle, low


def store_level(message_ref, row, level):
    for i, part in enumerate(split_level(level)):
        message_ref[row, :, i * LANES : (i + 1) * LANES] = part


def load_level(message_ref, row):
    parts = [
        message_ref[row, :, i * LANES : (i + 1) * LANES].astype(jnp.float32) for i in range(3)
    ]
    return (parts[0] + parts[1]) + parts[2]


def load_kernel(first, here_ref, cache_ref, after_ref, out_ref, sem):
    copy = pltpu.make_async_copy(cache_ref.at[pl.ds(first, out_ref.shape[0])], out_ref, sem)
    copy.start()
    copy.wait()


def load(here, cache, part, parts, after):
    pages = cache.shape[0] // parts
    return pl.pallas_call(
        functools.partial(load_kernel, part * pages),
        out_shape=pltpu.VMEM((pages, *cache.shape[1:]), cache.dtype),
        in_specs=[
            SMEM_SPEC,
            pl.BlockSpec(memory_space=pltpu.HBM),
            pl.BlockSpec(memory_space=pl.ANY),
        ],
        out_specs=VMEM_SPEC,
        scratch_shapes=[pltpu.SemaphoreType.DMA],
        compiler_params=pltpu.CompilerParams(vmem_limit_bytes=MIB),
        cost_estimate=pl.CostEstimate(
            flops=0, bytes_accessed=2 * cache.size // parts, transcendentals=0
        ),
        name="load",
    )(here, pltpu.with_memory_space_constraint(cache, pltpu.HBM), after)


def gate_kernel(block_ref, after_ref, out_ref):
    pass


def gate(block, after):
    return pl.pallas_call(
        gate_kernel,
        out_shape=jax.ShapeDtypeStruct(block.shape, block.dtype),
        in_specs=[pl.BlockSpec(memory_space=pl.ANY)] * 2,
        out_specs=pl.BlockSpec(memory_space=pl.ANY),
        input_output_aliases={0: 0},
        compiler_params=pltpu.CompilerParams(vmem_limit_bytes=MIB),
        cost_estimate=pl.CostEstimate(flops=0, bytes_accessed=0, transcendentals=0),
        name="gate",
    )(block, after)


def attend_kernel(score_scale, steps, blocks, owner_ref, weight_ref, *refs):
    cache_refs, refs = refs[:CACHE_PARTS], refs[CACHE_PARTS:]
    query_refs, message_refs = refs[:blocks], refs[blocks : 2 * blocks]
    weight_out, query_scr, score_scr, max_scr, total_scr, sum_scr, weight_sem = refs[2 * blocks :]
    requests, heads, entry_size = query_scr.shape
    pages_part, page_len, _ = cache_refs[0].shape
    _, heads_here, latent_size = message_refs[0].shape
    rope_size = entry_size - latent_size
    ropes_row = latent_size // rope_size
    pair_len = 2 * page_len
    pair_count = GROUP_PAGES // 2
    groups_part = pages_part // GROUP_PAGES
    groups_step = groups_part // steps
    group_len = GROUP_PAGES * page_len

    weight_copy = pltpu.make_async_copy(weight_ref, weight_out, weight_sem)
    weight_copy.start()

    for b, ref in enumerate(query_refs):
        rows = slice(b * heads_here, (b + 1) * heads_here)
        for r in range(requests):
            start = r % ropes_row * rope_size
            query_scr[r, rows, :latent_size] = ref[r]
            query_scr[r, rows, latent_size:] = ref[requests + r // ropes_row][
                :, start : start + rope_size
            ]

    first_half = lax.broadcasted_iota(jnp.int32, (heads, pair_len), 1) < page_len

    for r in range(requests + 1):
        max_scr[r] = jnp.full((heads, pair_len), masked_score, jnp.float32)
        total_scr[r] = jnp.zeros((heads, pair_len), jnp.float32)
        sum_scr[r] = jnp.zeros((heads, latent_size), jnp.float32)

    def owners_of(g):
        raw = [owner_ref[g * GROUP_PAGES + k] for k in range(GROUP_PAGES)]
        return [jnp.where(o < 0, requests, o) for o in raw]

    def score_group(part, local):
        g = part * groups_part + local
        owners = owners_of(g)
        keys = cache_refs[part][pl.ds(local * GROUP_PAGES, GROUP_PAGES)].reshape(group_len, entry_size)
        queries = jnp.concatenate(
            [query_scr[jnp.minimum(o, requests - 1)] for o in owners], axis=0
        )
        scores = lax.dot_general(
            queries, keys, (((1,), (1,)), ((), ())), preferred_element_type=jnp.float32
        )
        for p in range(pair_count):
            left, right = 2 * p, 2 * p + 1
            columns = slice(p * pair_len, (p + 1) * pair_len)
            pair = score_scale * jnp.where(
                first_half,
                scores[left * heads : (left + 1) * heads, columns],
                scores[right * heads : (right + 1) * heads, columns],
            )
            score_scr[g * pair_count + p] = pair
            max_scr[owners[left]] = jnp.maximum(
                max_scr[owners[left]], jnp.where(first_half, pair, masked_score)
            )
            max_scr[owners[right]] = jnp.maximum(
                max_scr[owners[right]], jnp.where(first_half, masked_score, pair)
            )

    def score_step(part, c, carry):
        for i in range(groups_step):
            score_group(part, c * groups_step + i)
        return carry

    for part in range(CACHE_PARTS):
        lax.fori_loop(0, steps, functools.partial(score_step, part), 0)

    for r in range(requests + 1):
        top = jnp.max(max_scr[r], axis=1, keepdims=True)
        max_scr[r] = jnp.broadcast_to(top, (heads, pair_len))

    def sum_group(part, local):
        g = part * groups_part + local
        owners = owners_of(g)
        values = cache_refs[part][pl.ds(local * GROUP_PAGES, GROUP_PAGES)].reshape(group_len, entry_size)[
            :, :latent_size
        ]
        rows = []
        for p in range(pair_count):
            left, right = owners[2 * p], owners[2 * p + 1]
            offset = jnp.where(first_half, max_scr[left], max_scr[right])
            weight = jnp.exp(score_scr[g * pair_count + p] - offset)
            left_weight = jnp.where(first_half, weight, 0.0)
            right_weight = jnp.where(first_half, 0.0, weight)
            total_scr[left] += left_weight
            total_scr[right] += right_weight
            for part in (left_weight, right_weight):
                half = part.astype(jnp.bfloat16)
                pieces = [half if q == p else jnp.zeros_like(half) for q in range(pair_count)]
                rows.append(jnp.concatenate(pieces, axis=1))
        added = jnp.dot(
            jnp.concatenate(rows, axis=0), values, preferred_element_type=jnp.float32
        )
        for k in range(GROUP_PAGES):
            sum_scr[owners[k]] += added[k * heads : (k + 1) * heads]

    def sum_step(part, c, carry):
        for i in range(groups_step):
            sum_group(part, c * groups_step + i)
        return carry

    for part in range(CACHE_PARTS):
        lax.fori_loop(0, steps, functools.partial(sum_step, part), 0)

    lane = lax.broadcasted_iota(jnp.int32, (heads, LANES), 1)
    stats = jnp.full((heads, LANES), masked_score, jnp.float32)
    for r in range(requests):
        total = jnp.sum(total_scr[r], axis=1, keepdims=True)
        present = total > 0.0
        safe = jnp.where(present, total, 1.0)
        mean = (sum_scr[r] * (1.0 / safe)).astype(jnp.bfloat16)
        level = jnp.where(present, max_scr[r][:, :1] + jnp.log(safe), masked_score)
        stats = jnp.where(lane == r, level, stats)
        for b in range(blocks):
            message_refs[b][r] = mean[b * heads_here : (b + 1) * heads_here]
    for b in range(blocks):
        message_refs[b][requests] = jnp.zeros((heads_here, latent_size), jnp.bfloat16)
        store_level(message_refs[b], requests, stats[b * heads_here : (b + 1) * heads_here])
    weight_copy.wait()


def attend(query_blocks, cache_parts, page_owner, output_weight, score_scale, latent_size):
    pages_part, page_len, entry_size = cache_parts[0].shape
    pages = pages_part * CACHE_PARTS
    blocks = len(query_blocks)
    heads_here = query_blocks[0].shape[1]
    requests = query_blocks[0].shape[0] * latent_size // entry_size
    heads = heads_here * blocks
    pair_len = 2 * page_len
    groups = pages_part // GROUP_PAGES
    steps = groups // max(d for d in range(1, 15) if groups % d == 0)
    out = pl.pallas_call(
        functools.partial(attend_kernel, score_scale, steps, blocks),
        out_shape=[
            pltpu.VMEM((requests + 1, heads_here, latent_size), jnp.bfloat16)
            for _ in range(blocks)
        ]
        + [pltpu.VMEM(output_weight.shape, output_weight.dtype)],
        in_specs=[SMEM_SPEC, pl.BlockSpec(memory_space=pl.ANY)]
        + [VMEM_SPEC] * (CACHE_PARTS + blocks),
        out_specs=[VMEM_SPEC] * (blocks + 1),
        scratch_shapes=[
            pltpu.VMEM((requests, heads, entry_size), jnp.bfloat16),
            pltpu.VMEM((pages // 2, heads, pair_len), jnp.float32),
            pltpu.VMEM((requests + 1, heads, pair_len), jnp.float32),
            pltpu.VMEM((requests + 1, heads, pair_len), jnp.float32),
            pltpu.VMEM((requests + 1, heads, latent_size), jnp.float32),
            pltpu.SemaphoreType.DMA,
        ],
        compiler_params=pltpu.CompilerParams(vmem_limit_bytes=16 * MIB),
        cost_estimate=pl.CostEstimate(
            flops=2 * pages * page_len * heads * (entry_size + latent_size) * 4,
            bytes_accessed=pages * page_len * entry_size * 2,
            transcendentals=pages * page_len * heads,
        ),
        name="attend",
    )(page_owner, output_weight, *map(in_vmem, [*cache_parts, *query_blocks]))
    return list(out[:-1]), out[-1]


def shares(levels):
    top = functools.reduce(jnp.maximum, levels)
    parts = [jnp.exp(level - top) for level in levels]
    total = functools.reduce(jnp.add, parts)
    return [part / total for part in parts], top + jnp.log(total)


def merge_kernel(own_ref, got_ref, out_ref):
    requests = own_ref.shape[0] - 1
    both = (own_ref, got_ref)
    weights, level = shares([load_level(ref, requests) for ref in both])
    for r in range(requests):
        out_ref[r] = sum(
            w[:, r : r + 1] * ref[r].astype(jnp.float32) for w, ref in zip(weights, both)
        ).astype(jnp.bfloat16)
    out_ref[requests] = jnp.zeros(out_ref.shape[1:], jnp.bfloat16)
    store_level(out_ref, requests, level)


def merge(own, got):
    return pl.pallas_call(
        merge_kernel,
        out_shape=pltpu.VMEM(own.shape, own.dtype),
        in_specs=[VMEM_SPEC] * 2,
        out_specs=VMEM_SPEC,
        compiler_params=pltpu.CompilerParams(vmem_limit_bytes=2 * MIB),
        cost_estimate=pl.CostEstimate(flops=4 * own.size, bytes_accessed=0, transcendentals=0),
        name="merge",
    )(in_vmem(own), in_vmem(got))


def finish_kernel(
    block_columns, count, here_ref, value_ref, weight_ref, *refs
):
    messages, (out_ref, attended_scr, head_scr) = refs[:-3], refs[-3:]
    requests, heads_here = messages[0].shape[0] - 1, messages[0].shape[1]
    value_size = value_ref.shape[2]
    owners, _, width = out_ref.shape
    weights, _ = shares([load_level(ref, requests) for ref in messages])
    for r in range(requests):
        attended_scr[r * heads_here : (r + 1) * heads_here] = sum(
            w[:, r : r + 1] * ref[r].astype(jnp.float32) for w, ref in zip(weights, messages)
        )
    attended = attended_scr[...].astype(jnp.bfloat16)
    row = lax.broadcasted_iota(jnp.int32, (requests, requests * heads_here), 0)
    column = lax.broadcasted_iota(jnp.int32, (requests, requests * heads_here), 1)
    for h in range(heads_here):
        pick = jnp.where(column == row * heads_here + h, 1.0, 0.0).astype(jnp.bfloat16)
        rows = jnp.dot(pick, attended, preferred_element_type=jnp.float32).astype(jnp.bfloat16)
        head_scr[:, h * value_size : (h + 1) * value_size] = jnp.dot(
            rows, value_ref[h], preferred_element_type=jnp.float32
        ).astype(jnp.bfloat16)
    head_out = head_scr[...]
    per_block = block_columns // width
    for j in range(owners // per_block):
        product = jnp.dot(
            head_out,
            weight_ref[:, j * block_columns : (j + 1) * block_columns],
            preferred_element_type=jnp.float32,
        ).astype(jnp.bfloat16)
        for i in range(per_block):
            ctx, head = divmod(j * per_block + i, owners // count)
            place = (here_ref[0] ^ head) * count + ctx
            out_ref[place] = product[:, i * width : (i + 1) * width]


def finish(here, messages, value_absorb, weight, count, owners):
    requests, heads_here = messages[0].shape[0] - 1, messages[0].shape[1]
    latent_size, value_size = value_absorb.shape[1:]
    depth, columns = weight.shape
    width = columns // owners
    block_columns = width
    while block_columns % LANES:
        block_columns *= 2
    return pl.pallas_call(
        functools.partial(finish_kernel, block_columns, count),
        out_shape=pltpu.VMEM((owners, requests, width), jnp.bfloat16),
        in_specs=[SMEM_SPEC] + [VMEM_SPEC] * (2 + len(messages)),
        out_specs=VMEM_SPEC,
        scratch_shapes=[
            pltpu.VMEM((requests * heads_here, latent_size), jnp.float32),
            pltpu.VMEM((requests, heads_here * value_size), jnp.bfloat16),
        ],
        compiler_params=pltpu.CompilerParams(vmem_limit_bytes=8 * MIB),
        cost_estimate=pl.CostEstimate(
            flops=2 * 256 * depth * columns, bytes_accessed=0, transcendentals=0
        ),
        name="finish",
    )(here, *[in_vmem(x) for x in (value_absorb, weight, *messages)])


def body(
    query_nope, query_rope, key_absorb, value_absorb, output_weight, latent_cache, page_owner
):
    requests, heads_here, nope_size = query_nope.shape
    latent_size = key_absorb.shape[2]
    rope_size = query_rope.shape[1] // heads_here
    score_scale = (nope_size + rope_size) ** (-0.5)
    count = lax.axis_size("ctx")
    cores = lax.axis_size("head")
    here = lax.axis_index("head").astype(jnp.int32).reshape(1)

    def exchange(x, distance):
        return lax.ppermute(x, "ctx", [(i, i ^ distance) for i in range(count)])

    query_latent = jnp.einsum(
        "rhn,hnl->rhl", query_nope, key_absorb, preferred_element_type=jnp.float32
    ).astype(jnp.bfloat16)
    ropes_row = latent_size // rope_size
    rope = query_rope.reshape(-1, ropes_row, heads_here, rope_size).transpose(0, 2, 1, 3)
    own = jnp.concatenate([query_latent, rope.reshape(-1, heads_here, latent_size)], axis=0)

    even = [*range(4, count, 2), *range(2, min(4, count), 2)]
    block_at = {distance: exchange(own, distance) for distance in [*even, 3, 1]}
    block_at[0] = own
    cache_parts = [load(here, latent_cache, 0, CACHE_PARTS, own)]
    for distance in even[:-1]:
        block_at[distance] = gate(block_at[distance], cache_parts[0])
        block_at[distance ^ 1] = exchange(block_at[distance], 1)
    for part in range(1, CACHE_PARTS):
        cache_parts.append(load(here, latent_cache, part, CACHE_PARTS, block_at[count - 2]))

    message_to, weight = attend(
        [block_at[d] for d in range(count)],
        cache_parts, page_owner, output_weight, score_scale, latent_size,
    )

    across = {distance: exchange(message_to[distance ^ 1], 1) for distance in [*even[:-1], 0]}
    direct = [exchange(message_to[distance], distance) for distance in (3, 2)]
    arrived = [
        exchange(merge(message_to[distance], across[distance]), distance)
        for distance in even[:-1]
    ]
    messages = [message_to[0], across[0], *direct, *arrived]
    pieces = finish(here, messages, value_absorb, weight, count, count * cores)
    total = pieces[:count].astype(jnp.float32)
    for distance in range(1, cores):
        got = lax.ppermute(
            pieces[distance * count : (distance + 1) * count],
            "head",
            [(i, i ^ distance) for i in range(cores)],
        )
        total = total + got.astype(jnp.float32)
    pieces = lax.all_to_all(
        total.astype(jnp.bfloat16), "ctx", split_axis=0, concat_axis=0, tiled=True
    )
    return jnp.sum(pieces.astype(jnp.float32), axis=0).astype(jnp.bfloat16)


def solution(mesh):
    return jax.shard_map(
        body,
        mesh=mesh,
        in_specs=(
            P("groups", ("ctx", "head"), None),
            P("groups", ("ctx", "head")),
            P(("ctx", "head"), None, None),
            P(("ctx", "head"), None, None),
            P(("ctx", "head"), None),
            P(("groups", "ctx"), None, None),
            P(("groups", "ctx")),
        ),
        out_specs=P("groups", ("ctx", "head")),
        check_vma=False,
    )
```
